128 devices in a mesh: dp: 8 (over y_hi, z), tensor: 16 (over y_lo, x, core).
Axes of the slice: x: 4, y: 4 (y_hi: 2, y_lo: 2; y = y_hi * 2 + y_lo), z: 4, core: 2. Of those that a mesh axis runs over, the one named last changes fastest.
Arguments:
- residual_in: bfloat16 [16384, 1024], P(('dp', 'tensor')), may hold values from -6 to 6
- row_lengths: int32 [8, 8], P('dp'), may hold values from 0 to 2048, as said below
- norm_gains: float32 [4, 1024], replicated, may hold values from 0.5 to 1.5
- query_weight: bfloat16 [1024, 1024], P('tensor'), may hold values from -0.1875 to 0.1875
- key_weight: bfloat16 [1024, 1024], P('tensor'), may hold values from -0.1875 to 0.1875
- value_weight: bfloat16 [1024, 1024], P('tensor'), may hold values from -0.1875 to 0.1875
- proj_weight: bfloat16 [1024, 1024], P('tensor'), may hold values from -0.75 to 0.75
- up_weight: bfloat16 [4096, 1024], P('tensor'), may hold values from -0.1875 to 0.1875
- down_weight: bfloat16 [4096, 1024], P('tensor'), may hold values from -0.09375 to 0.09375
- upstream: bfloat16 [16384, 1024], P(('dp', 'tensor')), may hold values from -6 to 6
Outputs:
- block_out: bfloat16 [16384, 1024], P(('dp', 'tensor'))
- input_grad: float32 [16384, 1024], P(('dp', 'tensor'))
- query_grad: float32 [1024, 1024], P('tensor')
- key_grad: float32 [1024, 1024], P('tensor')
- value_grad: float32 [1024, 1024], P('tensor')
- proj_grad: float32 [1024, 1024], P('tensor')
- up_grad: float32 [4096, 1024], P('tensor')
- down_grad: float32 [4096, 1024], P('tensor')
- gains_grad: float32 [4, 1024], replicated
- branch_stats: float32 [2], replicated
The draws below stay inside these ranges and needn't reach their ends.
Inputs may be any that keep to these rules, and one draw needn't show every extreme that they name: `row_lengths`: in half of the groups (which ones drawn from the seed) the first entry is 2048 and the others 0: one row fills the group. In the other groups the 8 entries lie in 0 to 512, sum to 2048, and one of them is exactly 512.
All inputs are finite; a program needn't handle non-finite values.
Results may differ from the reference program's by a relative error of at most 0.025.
Values may be sent and summed in bfloat16 or wider, within the bound.
No kernel may reach another device: no remote copies, remote signals or barrier semaphores. Data moves between devices by JAX's collectives and lax.ppermute only.
A program may use at most 128 MiB of HBM per device.

```python
import jax
import jax.numpy as jnp
from jax import lax

D = 1024
HEADS = 16
HEAD_DIM = 64
FF = 4096
SHORT = 512
BLOCK = 512
SEQ = 2048
GROUPS = 8
TOKENS = 16384
SLOTS = 8


def draw_row_lengths(key, part):
    key_kind = jax.random.fold_in(key, 11)
    key_pair = jax.random.fold_in(key, 12)
    key_full = jax.random.fold_in(key, 13)
    key_order = jax.random.fold_in(key, 14)
    half_len = SHORT // 2
    pair_count = SLOTS // 2
    shifts = jax.random.randint(key_pair, (GROUPS, pair_count), -(half_len - 1), half_len)
    full_pair = jax.random.randint(key_full, (GROUPS,), 0, pair_count)
    shifts = jnp.where(jnp.arange(pair_count)[None, :] == full_pair[:, None], half_len, shifts)
    first_len = half_len + shifts
    second_len = half_len - shifts
    short_rows = jnp.stack([first_len, second_len], axis=-1).reshape(GROUPS, SLOTS)
    order_keys = jax.random.split(key_order, GROUPS)
    orders = jax.vmap(lambda one_key: jax.random.permutation(one_key, SLOTS))(order_keys)
    short_rows = jnp.take_along_axis(short_rows, orders, axis=1)
    long_rows = jnp.where(jnp.arange(SLOTS)[None, :] == 0, SEQ, 0) + jnp.zeros((GROUPS, 1), jnp.int32)
    ranking = jax.random.permutation(key_kind, GROUPS)
    is_long = (ranking < GROUPS // 2)[:, None]
    return jnp.where(is_long, long_rows, short_rows).astype(jnp.int32)


def level_of(own_key, dims, cuts, smallest, largest):
    def one(dim, shards_of):
        steps = jax.random.uniform(jax.random.fold_in(jax.random.fold_in(own_key, 6), dim), (shards_of,), jnp.float32, smallest / len(cuts), largest / len(cuts))
        return jnp.repeat(jnp.exp(steps), dims[dim] // shards_of).reshape((-1,) + (1,) * (len(dims) - dim - 1))

    factor_of = one(*cuts[0])
    for cut in cuts[1:]:
        factor_of = factor_of * one(*cut)
    return factor_of


def normal_values(own_key, extent, scale, reach, shards=(), held_as=jnp.bfloat16):
    values = jax.random.normal(own_key, extent, jnp.float32) * scale
    if len(shards) > 0:
        values = level_of(own_key, extent, shards, -0.22, 0.18) * values
    return jnp.clip(values, min=-reach, max=reach).astype(held_as)


def setup_inputs(seed: int = 0) -> dict:
    keys = jax.random.split(jax.random.key(seed), 11)
    residual_in = normal_values(keys[0], (TOKENS, D), 1.0, 6.0, ((0, 128),))
    row_lengths = draw_row_lengths(jax.random.fold_in(keys[10], 71), 0)
    norm_gains = jnp.clip(1.0 + 0.1 * jax.random.normal(keys[2], (4, D), jnp.float32), 0.5, 1.5)
    query_weight = normal_values(keys[3], (D, D), D ** -0.5, 0.1875, ((0, 16),))
    key_weight = normal_values(keys[4], (D, D), D ** -0.5, 0.1875, ((0, 16),))
    value_weight = normal_values(keys[5], (D, D), D ** -0.5, 0.1875, ((0, 16),))
    proj_weight = normal_values(keys[6], (D, D), HEAD_DIM ** -0.5, 0.75, ((0, 16),))
    up_weight = normal_values(keys[7], (FF, D), D ** -0.5, 0.1875, ((0, 16),))
    down_weight = normal_values(keys[8], (FF, D), FF ** -0.5, 0.09375, ((0, 16),))
    upstream = normal_values(keys[9], (TOKENS, D), 1.0, 6.0, ((0, 128),))
    return {"residual_in": residual_in, "row_lengths": row_lengths, "norm_gains": norm_gains, "query_weight": query_weight, "key_weight": key_weight, "value_weight": value_weight, "proj_weight": proj_weight, "up_weight": up_weight, "down_weight": down_weight, "upstream": upstream}


@jax.custom_vjp
def low(v):
    return lax.optimization_barrier(v.astype(jnp.bfloat16)).astype(jnp.float32)

@jax.custom_vjp
def low_back(v):
    return v

def low_keep(v):
    return (low(v), None)

def low_pass(kept, grad):
    return (grad,)

def back_keep(v):
    return (v, None)

def back_low(kept, grad):
    return (low(grad),)
low.defvjp(low_keep, low_pass)
low_back.defvjp(back_keep, back_low)

def layer_norm(values, scale_gain):
    center = values - lax.optimization_barrier(jnp.mean(values, axis=-1, keepdims=True))
    spread = lax.optimization_barrier(jnp.mean(center * center, axis=-1, keepdims=True))
    return center * lax.rsqrt(spread + 1e-05) * scale_gain

def row_layout(lengths, seq_total):
    row_end = jnp.cumsum(lengths).astype(jnp.int32)
    row_begin = (row_end - lengths).astype(jnp.int32)
    places = jnp.arange(seq_total, dtype=jnp.int32)
    row_ids = lax.optimization_barrier(jnp.sum((row_end[None, :] <= places[:, None]).astype(jnp.int32), axis=1)).astype(jnp.int32)
    slot_ids = jnp.arange(lengths.shape[0], dtype=jnp.int32)
    row_start = lax.optimization_barrier(jnp.sum(jnp.where(row_ids[:, None] == slot_ids[None, :], row_begin[None, :], 0), axis=1)).astype(jnp.int32)
    return (row_ids, (places - row_start).astype(jnp.int32), row_start)

def rope_tables(positions, head_width):
    half_width = head_width // 2
    frequency = 10000.0 ** (-2.0 * jnp.arange(half_width, dtype=jnp.float32) / head_width)
    angles = positions.astype(jnp.float32)[:, None] * frequency[None, :]
    cosine = jnp.concatenate([jnp.cos(angles), jnp.cos(angles)], axis=1)
    sine_table = jnp.concatenate([jnp.sin(angles), jnp.sin(angles)], axis=1)
    return (cosine, sine_table)

def rotate(field, cosine, sine_table):
    half_width = field.shape[-1] // 2
    turned = jnp.concatenate([-field[..., half_width:], field[..., :half_width]], axis=-1)
    return field * cosine[:, None, :] + turned * sine_table[:, None, :]

def attend(query_rot, key_rot, value_low, row_ids):
    highest = lax.Precision.HIGHEST
    score_scale = HEAD_DIM ** (-0.5)
    places = jnp.arange(SEQ, dtype=jnp.int32)

    def one_block(query_block):
        query_first = query_block * BLOCK
        query_part = lax.dynamic_slice_in_dim(query_rot, query_first, BLOCK, 0)
        query_rows = lax.dynamic_slice_in_dim(row_ids, query_first, BLOCK, 0)
        query_places = query_first + jnp.arange(BLOCK, dtype=jnp.int32)
        visible = (query_rows[:, None] == row_ids[None, :]) & (places[None, :] <= query_places[:, None])
        raw_scores = jnp.einsum('qhd,khd->hqk', query_part, key_rot, precision=highest)
        scores = low_back(jnp.where(visible[None], raw_scores * score_scale, -1e+30))
        peak_score = lax.optimization_barrier(jnp.max(scores, axis=-1, keepdims=True))
        log_total = peak_score + jnp.log(lax.optimization_barrier(jnp.sum(jnp.exp(scores - peak_score), axis=-1, keepdims=True)))
        weights = low(jnp.exp(scores - log_total))
        return jnp.einsum('hqk,khd->qhd', weights, value_low, precision=highest)
    blocks = lax.map(jax.checkpoint(one_block), jnp.arange(SEQ // BLOCK, dtype=jnp.int32))
    return blocks.reshape(SEQ, HEADS, HEAD_DIM)

def one_group(field, lengths, gain_rows, query_mat, key_mat, value_mat, proj_mat, up_mat, down_mat):
    highest = lax.Precision.HIGHEST
    row_ids, positions, row_start = row_layout(lengths, SEQ)
    cosine, sine_table = rope_tables(positions, HEAD_DIM)
    first_norm = low(layer_norm(field, gain_rows[0]))
    query = jnp.dot(first_norm, query_mat.T, precision=highest).reshape(SEQ, HEADS, HEAD_DIM)
    keyed = jnp.dot(first_norm, key_mat.T, precision=highest).reshape(SEQ, HEADS, HEAD_DIM)
    valued = jnp.dot(first_norm, value_mat.T, precision=highest).reshape(SEQ, HEADS, HEAD_DIM)
    query_rot = low(rotate(low_back(query), cosine, sine_table))
    key_rot = low(rotate(low_back(keyed), cosine, sine_table))
    value_low = low(low_back(valued))
    attended = attend(query_rot, key_rot, value_low, row_ids).reshape(SEQ, D)
    attended = low(low_back(attended))
    attn_pre = low_back(jnp.dot(attended, proj_mat, precision=highest))
    middle = field + layer_norm(attn_pre, gain_rows[1])
    second_norm = low(layer_norm(middle, gain_rows[2]))
    lifted = low_back(jnp.dot(second_norm, up_mat.T, precision=highest))
    active = low(jax.nn.gelu(lifted, approximate=True))
    mlp_pre = low_back(jnp.dot(active, down_mat, precision=highest))
    output = middle + layer_norm(mlp_pre, gain_rows[3])
    branch_stat = jnp.stack([jnp.sum(lax.optimization_barrier(jnp.mean(attn_pre * attn_pre, axis=-1))), jnp.sum(lax.optimization_barrier(jnp.mean(mlp_pre * mlp_pre, axis=-1)))])
    return (output, branch_stat)

def reference(residual_in, row_lengths, norm_gains, query_weight, key_weight, value_weight, proj_weight, up_weight, down_weight, upstream):

    def forward(inputs_all, gain_rows, query_mat, key_mat, value_mat, proj_mat, up_mat, down_mat):

        def group_step(carried, pieces):
            field, lengths = pieces
            output, branch_stat = one_group(field, lengths, gain_rows, query_mat, key_mat, value_mat, proj_mat, up_mat, down_mat)
            return (carried + branch_stat, output)
        totals, outputs = lax.scan(jax.checkpoint(group_step), jnp.zeros((2,), jnp.float32), (inputs_all.reshape(GROUPS, SEQ, D), row_lengths))
        return (outputs.reshape(TOKENS, D), totals / TOKENS)
    primals = (residual_in.astype(jnp.float32), norm_gains.astype(jnp.float32), query_weight.astype(jnp.float32), key_weight.astype(jnp.float32), value_weight.astype(jnp.float32), proj_weight.astype(jnp.float32), up_weight.astype(jnp.float32), down_weight.astype(jnp.float32))
    result, pullback, stats = jax.vjp(forward, *primals, has_aux=True)
    gradients = pullback(upstream.astype(jnp.float32))
    return (result.astype(jnp.bfloat16), gradients[0], gradients[2], gradients[3], gradients[4], gradients[5], gradients[6], gradients[7], gradients[1], stats)
```

```python
import functools

import jax
import jax.numpy as jnp
import numpy as np
from jax import lax
from jax.experimental import pallas as pl
from jax.experimental.pallas import tpu as pltpu
from jax.sharding import Mesh
from jax.sharding import PartitionSpec as P

D = 1024
T = 128
NB = 8
OWN = NB * T
F32 = jnp.float32
BF16 = jnp.bfloat16
NEG = -1e30
EPS = 1e-05
RIGHT = [(i, (i + 1) % 4) for i in range(4)]
LEFT = [(i, (i + 3) % 4) for i in range(4)]
SWAP = [(0, 1), (1, 0)]
OUTER = [(0, 3), (3, 0), (1, 2), (2, 1)]
PAIR1 = [(0, 1), (1, 0), (2, 3), (3, 2)]
PAIR2 = [(0, 2), (2, 0), (1, 3), (3, 1)]
NT = (((1,), (1,)), ((), ()))
NN = (((1,), (0,)), ((), ()))
TN = (((0,), (0,)), ((), ()))
GELU_A = float(np.sqrt(2.0 / np.pi))
GELU_B = 0.044715


def mm(a, b, dims=NN):
    return lax.dot_general(a, b, dims, preferred_element_type=F32)


def call(body, outs, n_smem, *args, scratch=(), vmem=56):
    in_specs = [pl.BlockSpec(memory_space=pltpu.SMEM)] * n_smem
    in_specs += [pl.BlockSpec(memory_space=pltpu.VMEM)] * (len(args) - n_smem)
    return pl.pallas_call(
        body,
        out_shape=tuple(jax.ShapeDtypeStruct(s, d) for s, d in outs),
        in_specs=in_specs,
        out_specs=tuple(pl.BlockSpec(memory_space=pltpu.VMEM) for _ in outs),
        scratch_shapes=list(scratch),
        compiler_params=pltpu.CompilerParams(vmem_limit_bytes=vmem << 20),
    )(*args)


def ring_gather(a, b, axis):
    la = lax.ppermute(a, axis, RIGHT)
    rb = lax.ppermute(b, axis, LEFT)
    lb = lax.ppermute(b, axis, RIGHT)
    ra = lax.ppermute(a, axis, LEFT)
    fa = lax.ppermute(la, axis, RIGHT)
    fb = lax.ppermute(rb, axis, LEFT)
    return [(a, b), (ra, rb), (fa, fb), (la, lb)]


def ring_scatter(parts, axis):
    (p0a, p0b), (p1a, p1b), (p2a, p2b), (p3a, p3b) = parts
    a1 = lax.ppermute(p2a, axis, RIGHT)
    b1 = lax.ppermute(p2b, axis, LEFT)
    a2 = lax.ppermute(p1b, axis, RIGHT)
    b2 = lax.ppermute(p3a, axis, LEFT)
    f1 = lax.ppermute(p1a + a1, axis, RIGHT)
    f2 = lax.ppermute(p3b + b1, axis, LEFT)
    return [p0a, b2, f1], [p0b, a2, f2]


def chip_gather(a, b):
    ab = jnp.concatenate([a, b], 0)
    y = lax.ppermute(ab, "yl", SWAP)
    near = ring_gather(a, b, "x")
    yl = lax.ppermute(y, "x", RIGHT)
    yr = lax.ppermute(y, "x", LEFT)
    fa = lax.ppermute(near[2][0], "yl", SWAP)
    fb = lax.ppermute(near[2][1], "yl", SWAP)
    h = a.shape[0]
    near = [jnp.concatenate(n, 0) for n in near]
    return near + [y, yr, jnp.concatenate([fa, fb], 0), yl]


def chip_scatter(parts):
    p = parts
    h = p[0].shape[0] // 2
    r1 = lax.ppermute(p[5], "x", RIGHT)
    l1 = lax.ppermute(p[7], "x", LEFT)
    y1 = lax.ppermute(p[6], "yl", SWAP)
    rb = lax.ppermute(p[1][h:], "x", RIGHT)
    la = lax.ppermute(p[3][:h], "x", LEFT)
    ra2 = lax.ppermute(p[2][:h] + y1[:h], "x", RIGHT)
    lb2 = lax.ppermute(p[2][h:] + y1[h:], "x", LEFT)
    y3 = lax.ppermute(p[4] + r1 + l1, "yl", SWAP)
    ra3 = lax.ppermute(p[1][:h] + ra2, "x", RIGHT)
    lb3 = lax.ppermute(p[3][h:] + lb2, "x", LEFT)
    return [p[0], y3], [la, ra3], [rb, lb3]


def norm_parts(v):
    center = v - jnp.mean(v, axis=-1, keepdims=True)
    inv = lax.rsqrt(jnp.mean(center * center, axis=-1, keepdims=True) + EPS)
    return center * inv, inv


def norm_back(vhat, inv, grad, gain):
    t = grad * gain
    return inv * (
        t
        - jnp.mean(t, axis=-1, keepdims=True)
        - vhat * jnp.mean(t * vhat, axis=-1, keepdims=True)
    )


def first_norm_kernel(x_ref, gains_ref, a_ref, b_ref):
    vhat, _ = norm_parts(x_ref[...].astype(F32))
    n = (vhat * gains_ref[0:1, :]).astype(BF16)
    a_ref[...] = n[: T // 2]
    b_ref[...] = n[T // 2 :]


def own_places(parity, rows):
    i = lax.broadcasted_iota(jnp.int32, (rows, T), 0)
    return ((i // T) * 2 + parity) * T + i % T


def row_of(ends_ref, places):
    row = jnp.zeros_like(places)
    start = jnp.zeros_like(places)
    end = jnp.int32(0)
    for k in range(8):
        end = end + ends_ref[0, k]
        inside = places >= end
        row = row + jnp.where(inside, 1, 0)
        start = jnp.where(inside, end, start)
    return row, places - start


def tables_kernel(idx_ref, len_ref, freq_ref, cos_ref, sin_ref, mq_ref, mk_ref, mko_ref):
    c = idx_ref[0]
    lane = lax.broadcasted_iota(jnp.int32, (OWN, T), 1)
    row, pos = row_of(len_ref, own_places(c, OWN))
    angle = pos.astype(F32) * freq_ref[...]
    cos_ref[...] = jnp.cos(angle)
    s = jnp.sin(angle)
    sin_ref[...] = jnp.where(lane % 64 < 32, -s, s)
    hot = jnp.where(lane == row, 1.0, 0.0)
    ones = jnp.where((lane >= 8) & (lane < 11), 1.0, 0.0)
    mq_ref[...] = jnp.where((lane < 8) & (lane != row), NEG, 0.0).astype(BF16)
    mk_ref[...] = (hot + ones).astype(BF16)
    row_o, _ = row_of(len_ref, own_places(1 - c, OWN))
    mko_ref[...] = (jnp.where(lane == row_o, 1.0, 0.0) + ones).astype(BF16)


def swap_halves(w):
    lane = lax.broadcasted_iota(jnp.int32, w.shape, 1)
    return jnp.where(lane % 64 < 32, pltpu.roll(w, 96, 1), pltpu.roll(w, 32, 1))


def pair_rows(c, own, other):
    first = jnp.where(c == 0, own, other)
    second = jnp.where(c == 0, other, own)
    return jnp.concatenate([first, second], 0)


def block_place(idx_ref, r):
    yl = idx_ref[1] if r < 4 else 1 - idx_ref[1]
    return yl * 4 + lax.rem(idx_ref[2] + r % 4, 4)


def qkv_kernel(idx_ref, *refs):
    blocks = refs[:8]
    own_ref, other_ref, cos_ref, sin_ref, q_ref, kv_ref, w_ref = refs[8:]
    c = idx_ref[0]
    w = jnp.concatenate(
        [
            pair_rows(c, own_ref[64 * i : 64 * i + 64], other_ref[64 * i : 64 * i + 64])
            for i in range(3)
        ],
        0,
    )
    w_ref[...] = w
    for r in range(8):
        rows = pl.ds(pl.multiple_of(block_place(idx_ref, r) * T, T), T)
        out = mm(blocks[r][...], w, NT)
        cos, sin = cos_ref[rows, :], sin_ref[rows, :]
        q, k = out[:, :T], out[:, T : 2 * T]
        q_ref[rows, :] = ((q * cos + swap_halves(q) * sin) * 0.125).astype(BF16)
        kv_ref[rows, :T] = (k * cos + swap_halves(k) * sin).astype(BF16)
        kv_ref[rows, T:] = out[:, 2 * T :].astype(BF16)


Q = 256


def head_lanes(w):
    lane = lax.broadcasted_iota(jnp.int32, w.shape, 1)
    zero = jnp.zeros_like(w)
    return jnp.where(lane < 64, w, zero), jnp.where(lane < 64, zero, w)


def diag_masks(c, queries_first):
    shape = (Q, Q)
    i = lax.broadcasted_iota(jnp.int32, shape, 0 if queries_first else 1)
    k = lax.broadcasted_iota(jnp.int32, shape, 1 if queries_first else 0)
    own = k <= i
    kb, ib = k // T, i // T
    other = (kb < ib) | ((kb == ib) & (c == 1))
    return own, other


def attend_kernel(idx_ref, q_ref, kv_ref, kvo_ref, mq_ref, mk_ref, mko_ref, o_ref, o32_ref, a0_ref, a1_ref):
    c = idx_ref[0]
    lane = lax.broadcasted_iota(jnp.int32, (Q, T), 1)
    masks = diag_masks(c, True)

    def query_tile(jt, carry):
        qrows = pl.ds(pl.multiple_of(jt * Q, Q), Q)
        mq = mq_ref[qrows, :]
        lhs = [jnp.concatenate([h, mq], 1) for h in head_lanes(q_ref[qrows, :])]

        def tile(it, state, diag):
            rows = pl.ds(pl.multiple_of(it * Q, Q), Q)
            out = []
            k_own = jnp.concatenate([kv_ref[rows, :T], mk_ref[rows, :]], 1)
            k_oth = jnp.concatenate([kvo_ref[rows, :T], mko_ref[rows, :]], 1)
            v_own = head_lanes(kv_ref[rows, T:])
            v_oth = head_lanes(kvo_ref[rows, T:])
            m, l, acc = state
            ms, ls, alphas, added = [], [], [], None
            for h in range(2):
                s1, s2 = mm(lhs[h], k_own, NT), mm(lhs[h], k_oth, NT)
                if diag:
                    s1 = jnp.where(masks[0], s1, NEG)
                    s2 = jnp.where(masks[1], s2, NEG)
                m_new = jnp.maximum(
                    m[h], jnp.max(jnp.maximum(s1, s2), axis=1, keepdims=True)
                )
                p1, p2 = jnp.exp(s1 - m_new), jnp.exp(s2 - m_new)
                alpha = jnp.exp(m[h] - m_new)
                ls.append(l[h] * alpha + jnp.sum(p1 + p2, axis=1, keepdims=True))
                ms.append(m_new)
                alphas.append(alpha)
                pv = mm(p1.astype(BF16), v_own[h]) + mm(p2.astype(BF16), v_oth[h])
                added = pv if added is None else added + pv
            acc = acc * jnp.where(lane < 64, alphas[0], alphas[1]) + added
            return tuple(ms), tuple(ls), acc

        col = lambda v: jnp.full((Q, 1), v, F32)
        state = ((col(NEG), col(NEG)), (col(0.0), col(0.0)), jnp.zeros((Q, T), F32))
        state = tile(jt, state, True)
        m, l, acc = lax.fori_loop(0, jt, lambda it, st: tile(it, st, False), state)
        o = acc / jnp.where(lane < 64, l[0], l[1])
        o32_ref[qrows, :] = o
        o_ref[qrows, :] = o.astype(BF16)
        for h, ref in enumerate((a0_ref, a1_ref)):
            ref[qrows, :] = split_lanes(m[h] + jnp.log(l[h]), lane) + mq
        return carry

    lax.fori_loop(0, OWN // Q, query_tile, 0)


def split_lanes(col, lane):
    hi = col.astype(BF16).astype(F32)
    mid = (col - hi).astype(BF16).astype(F32)
    low = col - hi - mid
    out = jnp.where(lane == 8, -hi, jnp.where(lane == 9, -mid, jnp.where(lane == 10, -low, 0.0)))
    return out.astype(BF16)


def middle_kernel(idx_ref, o_ref, *refs):
    wos = refs[:8], refs[8:16]
    x_ref, gains_ref, a_ref, h_ref, n2a_ref, n2b_ref, full_ref, wo_ref, stat_ref = refs[16:]
    c = idx_ref[0]
    for r in range(8):
        j = block_place(idx_ref, r)
        rows = pl.ds(pl.multiple_of(j * T, T), T)
        wo_ref[rows, :] = pair_rows(c, wos[0][r][...], wos[1][r][...])
    o = jnp.concatenate([o_ref[j] for j in range(8)], 1)
    full_ref[...] = o
    a = mm(o, wo_ref[...])
    a_ref[...] = a
    vhat, _ = norm_parts(a)
    h = x_ref[...].astype(F32) + vhat * gains_ref[1:2, :]
    h_ref[...] = h
    vhat, _ = norm_parts(h)
    n = (vhat * gains_ref[2:3, :]).astype(BF16)
    n2a_ref[...] = n[: T // 2]
    n2b_ref[...] = n[T // 2 :]
    stat_ref[...] = jnp.zeros((8, T), F32) + jnp.sum(a * a) * (1.0 / D)


def gelu_tanh(u):
    return jnp.tanh(GELU_A * (u + GELU_B * u * u * u))


def mlp_forward_kernel(*refs):
    ns, ws = refs[:8], refs[8:12]
    u_ref, outs = refs[12], refs[13:21]
    n = jnp.concatenate([r[...] for r in ns], 0)
    m = jnp.zeros((4 * T, D), F32)
    for s in range(4):
        u = mm(n, ws[s][:256], NT)
        u_ref[:, 256 * s : 256 * s + 256] = u
        z = (0.5 * u * (1.0 + gelu_tanh(u))).astype(BF16)
        m = m + mm(z, ws[s][256:])
    for i in range(8):
        outs[i][...] = m[64 * i : 64 * i + 64].astype(BF16)


def turn_kernel(*refs):
    (a0, a1, a2, b0, b1, b2, h_ref, gains_ref, up_ref, out_ref, ga_ref, gb_ref, dc_ref, stat_ref) = refs
    add = lambda p, q, r: p[...].astype(F32) + q[...].astype(F32) + r[...].astype(F32)
    m = jnp.concatenate([add(a0, a1, a2), add(b0, b1, b2)], 0)
    vhat, inv = norm_parts(m)
    gain = gains_ref[3:4, :]
    out_ref[...] = (h_ref[...] + vhat * gain).astype(BF16)
    dy = up_ref[...].astype(F32)
    dc_ref[...] = jnp.sum(dy * vhat, axis=0, keepdims=True)
    g = norm_back(vhat, inv, dy, gain).astype(BF16)
    ga_ref[...] = g[: T // 2]
    gb_ref[...] = g[T // 2 :]
    stat_ref[...] = jnp.zeros((8, T), F32) + jnp.sum(m * m) * (1.0 / D)


def mlp_backward_kernel(*refs):
    gs, ws = refs[:8], refs[8:12]
    u_ref, z_ref, du_ref, outs = refs[12], refs[13], refs[14], refs[15:23]
    g = jnp.concatenate([r[...] for r in gs], 0)
    dn = jnp.zeros((4 * T, D), F32)
    for s in range(4):
        cols = slice(256 * s, 256 * s + 256)
        u = u_ref[:, cols]
        t = gelu_tanh(u)
        z_ref[:, cols] = (0.5 * u * (1.0 + t)).astype(BF16)
        slope = 0.5 * (1.0 + t) + 0.5 * u * (1.0 - t * t) * GELU_A * (1.0 + 3.0 * GELU_B * u * u)
        du = (mm(g, ws[s][256:], NT) * slope).astype(BF16)
        du_ref[:, cols] = du
        dn = dn + mm(du, ws[s][:256])
    for i in range(8):
        outs[i][...] = dn[64 * i : 64 * i + 64].astype(BF16)


def mlp_grads_kernel(*refs):
    ns, gs, z_ref, du_ref, keep_ref, send_ref = refs[:8], refs[8:16], *refs[16:]
    n = jnp.concatenate([r[...] for r in ns], 0)
    g = jnp.concatenate([r[...] for r in gs], 0)
    for s, (ref, slot) in enumerate(((keep_ref, 0), (send_ref, 0), (keep_ref, 1), (send_ref, 1))):
        cols = slice(256 * s, 256 * s + 256)
        ref[slot, :256] = mm(du_ref[:, cols], n, TN).astype(BF16)
        ref[slot, 256:] = mm(z_ref[:, cols], g, TN).astype(BF16)


def back_middle_kernel(*refs):
    (a0, a1, a2, b0, b1, b2, h_ref, a_ref, gains_ref, up_ref, wo_ref, dh_ref, ga_ref, do_ref, dc_ref) = refs
    add = lambda p, q, r: p[...].astype(F32) + q[...].astype(F32) + r[...].astype(F32)
    dn = jnp.concatenate([add(a0, a1, a2), add(b0, b1, b2)], 0)
    vhat, inv = norm_parts(h_ref[...])
    dc_ref[1:2, :] = jnp.sum(dn * vhat, axis=0, keepdims=True)
    dh = up_ref[...].astype(F32) + norm_back(vhat, inv, dn, gains_ref[2:3, :])
    dh_ref[...] = dh
    vhat, inv = norm_parts(a_ref[...])
    dc_ref[0:1, :] = jnp.sum(dh * vhat, axis=0, keepdims=True)
    ga = norm_back(vhat, inv, dh, gains_ref[1:2, :]).astype(BF16)
    ga_ref[...] = ga
    do = mm(ga, wo_ref[...], NT).astype(BF16)
    for j in range(8):
        do_ref[j] = do[:, T * j : T * j + T]


def attend_back_kernel(idx_ref, q_ref, kv_ref, kvo_ref, do_ref, o_ref, mk_ref, mko_ref, a0_ref, a1_ref, cos_ref, sin_ref, dq_ref, own_ref, oth_ref, accq, acco):
    c = idx_ref[0]
    lane = lax.broadcasted_iota(jnp.int32, (Q, T), 1)
    masks = diag_masks(c, False)
    own_ref[...] = jnp.zeros_like(own_ref)
    acco[...] = jnp.zeros_like(acco)

    def query_tile(jt, carry):
        qrows = pl.ds(pl.multiple_of(jt * Q, Q), Q)
        do = do_ref[qrows, :]
        q_h, do_h = head_lanes(q_ref[qrows, :]), head_lanes(do)
        inner = do.astype(F32) * o_ref[qrows, :]
        qa, da = [], []
        for h, ref in enumerate((a0_ref, a1_ref)):
            delta = jnp.sum(jnp.where((lane < 64) == (h == 0), inner, 0.0), axis=1, keepdims=True)
            qa.append(jnp.concatenate([q_h[h], ref[qrows, :]], 1))
            da.append(jnp.concatenate([do_h[h], split_lanes(delta, lane)], 1))
        q_st, do_st = jnp.concatenate(q_h, 0), jnp.concatenate(do_h, 0)

        def side(rows, kv, mk, acc, mask):
            k, v, m = kv[rows, :T], kv[rows, T:], mk[rows, :]
            ka, va = jnp.concatenate([k, m], 1), jnp.concatenate([v, m], 1)
            k_h = head_lanes(k)
            ps, ss, dq = [], [], None
            for h in range(2):
                p = jnp.exp(mm(ka, qa[h], NT))
                if mask is not None:
                    p = jnp.where(mask, p, 0.0)
                s = (p * mm(va, da[h], NT)).astype(BF16)
                ps.append(p.astype(BF16))
                ss.append(s)
                part = mm(s, k_h[h], TN)
                dq = part if dq is None else dq + part
            acc[rows, :T] += mm(jnp.concatenate(ss, 1), q_st)
            acc[rows, T:] += mm(jnp.concatenate(ps, 1), do_st)
            return dq

        def tile(it, diag):
            rows = pl.ds(pl.multiple_of(it * Q, Q), Q)
            return side(rows, kv_ref, mk_ref, own_ref, masks[0] if diag else None) + side(
                rows, kvo_ref, mko_ref, acco, masks[1] if diag else None
            )

        accq[...] = tile(jt, True)

        def step(it, carry):
            accq[...] += tile(it, False)
            return carry

        lax.fori_loop(0, jt, step, 0)
        dq = accq[...] * 0.125
        dq_ref[qrows, :] = (
            dq * cos_ref[qrows, :] + swap_halves(dq * sin_ref[qrows, :])
        ).astype(BF16)
        return carry

    lax.fori_loop(0, OWN // Q, query_tile, 0)
    oth_ref[...] = acco[...].astype(BF16)


def input_back_kernel(idx_ref, dq_ref, own_ref, recv_ref, w_ref, cos_ref, sin_ref, g_ref, *outs):
    both = own_ref[...] + recv_ref[...].astype(F32)
    dk = both[:, :T]
    g_ref[:, :T] = dq_ref[...]
    g_ref[:, T : 2 * T] = (dk * cos_ref[...] + swap_halves(dk * sin_ref[...])).astype(BF16)
    g_ref[:, 2 * T :] = both[:, T:].astype(BF16)
    for r in range(8):
        rows = pl.ds(pl.multiple_of(block_place(idx_ref, r) * T, T), T)
        outs[r][...] = mm(g_ref[rows, :], w_ref[...]).astype(BF16)


def attn_grads_kernel(idx_ref, g_ref, *refs):
    ns = refs[:8]
    w_ref, gains_ref, own_ref, send_ref, dc_ref, scr = refs[8:]
    c = idx_ref[0]
    for r in range(8):
        scr[pl.ds(pl.multiple_of(block_place(idx_ref, r) * T, T), T), :] = ns[r][...]
    dc = jnp.zeros((1, D), F32)
    for i in range(3):
        w = mm(g_ref[:, T * i : T * i + T], scr[...], TN)
        dc = dc + jnp.sum(w * w_ref[T * i : T * i + T, :].astype(F32), axis=0, keepdims=True)
        own_ref[64 * i : 64 * i + 64] = jnp.where(c == 0, w[:64], w[64:]).astype(BF16)
        send_ref[64 * i : 64 * i + 64] = jnp.where(c == 0, w[64:], w[:64]).astype(BF16)
    dc_ref[...] = dc / gains_ref[0:1, :]


def proj_grads_kernel(idx_ref, o_ref, ga_ref, *outs):
    c = idx_ref[0]
    w = mm(o_ref[...], ga_ref[...], TN)
    scr = outs[-1]
    scr[...] = w
    for r in range(8):
        base = block_place(idx_ref, r) * T
        own = pl.ds(pl.multiple_of(base + c * 64, 64), 64)
        oth = pl.ds(pl.multiple_of(base + (1 - c) * 64, 64), 64)
        outs[0][r] = scr[own, :].astype(BF16)
        outs[1][r] = scr[oth, :].astype(BF16)


def last_kernel(p0, y3, la, ra, rb, lb, x_ref, dh_ref, gains_ref, out_ref):
    h = T // 2
    f = lambda r: r[...].astype(F32)
    dn = f(p0) + f(y3) + jnp.concatenate([f(la) + f(ra), f(rb) + f(lb)], 0)
    vhat, inv = norm_parts(x_ref[...].astype(F32))
    out_ref[...] = dh_ref[...] + norm_back(vhat, inv, dn, gains_ref[0:1, :])


def half_blocks(g, z):
    n = g.shape[0] // 4
    out = []
    for r in range(4):
        first = lax.rem(z + r, 4) * n
        out.append(
            (
                lax.dynamic_slice_in_dim(g, first, n // 2, 0),
                lax.dynamic_slice_in_dim(g, first + n // 2, n // 2, 0),
            )
        )
    return out


def sum_terms(terms):
    out = terms[0].astype(F32)
    for t in terms[1:]:
        out = out + t.astype(F32)
    return out.astype(BF16)


def data_sum(g, z):
    ta, tb = ring_scatter(half_blocks(g, z), "z")
    ab = jnp.concatenate([sum_terms(ta), sum_terms(tb)], 0)
    ab = ab + lax.ppermute(ab, "yh", SWAP)
    h = ab.shape[0] // 2
    blocks = ring_gather(ab[:h], ab[h:], "z")
    out = jnp.zeros(g.shape, F32)
    n = g.shape[0] // 4
    for r in range(4):
        blk = jnp.concatenate(blocks[r], 0).astype(F32)
        out = lax.dynamic_update_slice_in_dim(out, blk, lax.rem(z + r, 4) * n, 0)
    return out


def on_device(x, lengths, gains, wq, wk, wv, wo, wup, wdown, upstream):
    c, yl, xi, z = (lax.axis_index(n) for n in ("c", "yl", "x", "z"))
    idx = jnp.stack([c, yl, xi, z]).astype(jnp.int32)
    freq = (10000.0 ** (-2.0 * np.arange(32) / 64.0)).astype(np.float32)
    freq = jnp.asarray(np.tile(freq, 4)[None, :])
    bf = lambda *s: (s, BF16)
    f32 = lambda *s: (s, F32)

    wqkv = jnp.concatenate([wq, wk, wv], 0)
    wqkv_o = lax.ppermute(wqkv, "c", SWAP)
    w_own = jnp.concatenate([wup, wdown], 0)
    w_core = lax.ppermute(w_own, "c", SWAP)
    w_y = lax.ppermute(w_own, ("yh", "yl"), OUTER)
    w_yc = lax.ppermute(w_y, "c", SWAP)
    ws = (w_own, w_core, w_y, w_yc)

    n1a, n1b = call(first_norm_kernel, [bf(64, D)] * 2, 0, x, gains)
    n1 = chip_gather(n1a, n1b)
    cos, sin, mq, mk, mko = call(
        tables_kernel, [f32(OWN, T)] * 2 + [bf(OWN, T)] * 3, 2, idx, lengths, freq
    )
    q, kv, w_pair = call(
        qkv_kernel, [bf(OWN, T), bf(OWN, 2 * T), bf(3 * T, D)], 1, idx, *n1, wqkv, wqkv_o, cos, sin
    )
    kvo = lax.ppermute(kv, "c", SWAP)
    wo_n = chip_gather(wo[:32], wo[32:])
    wo_c = lax.ppermute(jnp.concatenate(wo_n, 0), "c", SWAP)
    wo_c = [wo_c[64 * r : 64 * r + 64] for r in range(8)]
    o, o32, a0, a1 = call(
        attend_kernel, [bf(OWN, T), f32(OWN, T), bf(OWN, T), bf(OWN, T)], 1, idx, q, kv, kvo, mq, mk, mko
    )
    o_all = lax.all_to_all(o.reshape(8, T, T), ("yl", "x"), 0, 0, tiled=True)
    a, h, n2a, n2b, o_full, wo_full, stat_a = call(
        middle_kernel,
        [f32(T, D), f32(T, D), bf(64, D), bf(64, D), bf(T, D), bf(D, D), f32(8, T)],
        1,
        idx,
        o_all,
        *wo_n,
        *wo_c,
        x,
        gains,
    )
    n2 = [v for pair in ring_gather(n2a, n2b, "x") for v in pair]
    u, *m_parts = call(mlp_forward_kernel, [f32(4 * T, D)] + [bf(64, D)] * 8, 0, *n2, *ws)
    ta, tb = ring_scatter([(m_parts[2 * i], m_parts[2 * i + 1]) for i in range(4)], "x")
    block_out, ga_, gb_, dc3, stat_m = call(
        turn_kernel,
        [bf(T, D), bf(64, D), bf(64, D), f32(1, D), f32(8, T)],
        0,
        *ta,
        *tb,
        h,
        gains,
        upstream,
    )
    gm = [v for pair in ring_gather(ga_, gb_, "x") for v in pair]
    zz, du, *d_parts = call(
        mlp_backward_kernel, [bf(4 * T, D), bf(4 * T, D)] + [bf(64, D)] * 8, 0, *gm, *ws, u
    )
    ta, tb = ring_scatter([(d_parts[2 * i], d_parts[2 * i + 1]) for i in range(4)], "x")
    keep, send = call(
        mlp_grads_kernel, [bf(2, 512, D), bf(2, 512, D)], 0, *n2, *gm, zz, du
    )
    dh, ga, do, dc12 = call(
        back_middle_kernel,
        [f32(T, D), bf(T, D), bf(8, T, T), f32(2, D)],
        0,
        *ta,
        *tb,
        h,
        a,
        gains,
        upstream,
        wo_full,
    )
    do_all = lax.all_to_all(do, ("yl", "x"), 0, 0, tiled=True).reshape(OWN, T)
    dq, own32, oth = call(
        attend_back_kernel,
        [bf(OWN, T), f32(OWN, 2 * T), bf(OWN, 2 * T)],
        1,
        idx,
        q,
        kv,
        kvo,
        do_all,
        o32,
        mk,
        mko,
        a0,
        a1,
        cos,
        sin,
        scratch=[pltpu.VMEM((Q, T), F32), pltpu.VMEM((OWN, 2 * T), F32)],
    )
    recv = lax.ppermute(oth, "c", SWAP)
    dqkv, *parts = call(
        input_back_kernel,
        [bf(OWN, 3 * T)] + [bf(T, D)] * 8,
        1,
        idx,
        dq,
        own32,
        recv,
        w_pair,
        cos,
        sin,
    )
    (p0, y3), (la, ra), (rb, lb) = chip_scatter(parts)
    g_own, g_send, dc0 = call(
        attn_grads_kernel,
        [bf(192, D), bf(192, D), f32(1, D)],
        1,
        idx,
        dqkv,
        *n1,
        w_pair,
        gains,
        scratch=[pltpu.VMEM((OWN, D), BF16)],
    )
    (input_grad,) = call(
        last_kernel, [f32(T, D)], 0, p0, y3, la, ra, rb, lb, x, dh, gains
    )

    got = lax.ppermute(send, "c", SWAP)
    mine, other = keep[0] + got[0], keep[1] + got[1]
    half = mine.shape[0] // 2
    inner = lax.ppermute(other[:half], "yl", SWAP)
    outer = lax.ppermute(other[half:], ("yh", "yl"), OUTER)
    mlp_grad = data_sum(mine + jnp.concatenate([inner, outer], 0), z)

    po, ps = call(
        proj_grads_kernel, [bf(8, 64, D), bf(8, 64, D)], 1, idx, o_full, ga,
        scratch=[pltpu.VMEM((D, D), F32)],
    )
    po = po + lax.ppermute(ps, "c", SWAP)
    (p0, y3), (la, ra), (rb, lb) = chip_scatter([po[r] for r in range(8)])
    proj = sum_terms([p0, y3, jnp.concatenate([la, rb], 0), jnp.concatenate([ra, lb], 0)])
    g_own = g_own + lax.ppermute(g_send, "c", SWAP)
    attn_grad = data_sum(jnp.concatenate([g_own, proj], 0), z)

    rows = jnp.concatenate(
        [
            dc0,
            dc12,
            dc3,
            jnp.zeros((1, D), F32) + stat_a[0:1, 0:1],
            jnp.zeros((1, D), F32) + stat_m[0:1, 0:1],
            jnp.zeros((2, D), F32),
        ],
        0,
    )
    for axis, perm in (
        ("c", SWAP),
        ("x", PAIR1),
        ("x", PAIR2),
        ("yl", SWAP),
        ("z", PAIR1),
        ("z", PAIR2),
        ("yh", SWAP),
    ):
        rows = rows + lax.ppermute(rows, axis, perm)
    stats = rows[4:6, 0] * (1.0 / 16384.0)
    return (
        block_out,
        input_grad,
        attn_grad[:64],
        attn_grad[64:128],
        attn_grad[128:192],
        attn_grad[192:],
        mlp_grad[:256],
        mlp_grad[256:],
        rows[:4],
        stats,
    )


def solution(mesh):
    names = ("yh", "z", "yl", "x", "c")
    fine = Mesh(np.asarray(mesh.devices).reshape(2, 4, 2, 4, 2), names)
    tokens, group, shard = P(names, None), P(("yh", "z"), None), P(("yl", "x", "c"), None)
    return jax.shard_map(
        on_device,
        mesh=fine,
        in_specs=(tokens, group, P(), shard, shard, shard, shard, shard, shard, tokens),
        out_specs=(tokens, tokens, shard, shard, shard, shard, shard, shard, P(), P()),
        check_vma=False,
    )
```

```python
import functools

import jax
import jax.numpy as jnp
import numpy as np
from jax import lax
from jax.experimental import pallas as pl
from jax.experimental.pallas import tpu as pltpu
from jax.sharding import Mesh
from jax.sharding import PartitionSpec as P

D = 1024
T = 128
NB = 8
OWN = NB * T
F32 = jnp.float32
BF16 = jnp.bfloat16
NEG = -1e30
EPS = 1e-05
MATCH = ([(0, 1), (1, 0), (2, 3), (3, 2)], [(1, 2), (2, 1), (3, 0), (0, 3)])
SIDE_A = [(2 * i + c, 2 * j + c) for c in range(2) for i, j in MATCH[c]]
SIDE_B = [(2 * i + c, 2 * j + c) for c in range(2) for i, j in MATCH[1 - c]]
SWAP = [(0, 1), (1, 0)]
OUTER = [(0, 3), (3, 0), (1, 2), (2, 1)]
NT = (((1,), (1,)), ((), ()))
NN = (((1,), (0,)), ((), ()))
TN = (((0,), (0,)), ((), ()))
GELU_A = float(np.sqrt(2.0 / np.pi))
GELU_B = 0.044715


def mm(a, b, dims=NN):
    return lax.dot_general(a, b, dims, preferred_element_type=F32)


class Load:
    def __init__(self, src, dst, sem):
        self.copy, self.dst, self.waited = pltpu.make_async_copy(src, dst, sem), dst, False
        self.copy.start()

    def ready(self):
        if not self.waited:
            self.copy.wait()
            self.waited = True
        return self.dst


class Store:
    def __init__(self, src, dst, sem):
        self.copy, self.ref, self.sent = pltpu.make_async_copy(src, dst, sem), src, False

    def flush(self):
        if not self.sent:
            self.copy.start()
            self.sent = True


def call(body, us, ins, outs, vmem=16, scratch=(), exports=0):
    space = {"S": pltpu.SMEM, "V": pltpu.VMEM, "H": pltpu.HBM, "X": pltpu.HBM, "R": pltpu.HBM}
    kinds_in, kinds_out = [k for k, _ in ins], [k for k, _, _ in outs]
    buffers = [pltpu.VMEM(a.shape, a.dtype) for k, a in ins if k == "H"]
    buffers += [pltpu.VMEM(s, d) for k, s, d in outs if k == "H"]
    n_sems = len(buffers) + exports

    def kernel(*refs):
        refs = list(refs)
        n_in, n_out = len(ins), len(outs)
        raw_in, raw_out = refs[:n_in], refs[n_in : n_in + n_out]
        held = refs[n_in + n_out : n_in + n_out + len(buffers)]
        rest = refs[n_in + n_out + len(buffers) :]
        if n_sems:
            sems, rest = rest[0], rest[1:]
        used = [0]
        exported = []

        def sem():
            used[0] += 1
            return sems.at[used[0] - 1]

        def export(src, dst):
            copy = pltpu.make_async_copy(src, dst, sem())
            copy.start()
            exported.append(copy)

        held = list(held)
        loads = [Load(r, held.pop(0), sem()) if k == "H" else r for k, r in zip(kinds_in, raw_in)]
        stores = [Store(held.pop(0), r, sem()) if k == "H" else r for k, r in zip(kinds_out, raw_out)]
        body(loads, stores, rest, export)
        for s in stores:
            if isinstance(s, Store):
                s.flush()
        for v in loads:
            if isinstance(v, Load):
                v.ready()
        for s in stores:
            if isinstance(s, Store):
                s.copy.wait()
        for copy in exported:
            copy.wait()

    return pl.pallas_call(
        kernel,
        out_shape=tuple(jax.ShapeDtypeStruct(s, d) for _, s, d in outs),
        in_specs=[pl.BlockSpec(memory_space=space[k]) for k in kinds_in],
        out_specs=tuple(pl.BlockSpec(memory_space=space[k]) for k in kinds_out),
        scratch_shapes=buffers + ([pltpu.SemaphoreType.DMA((n_sems,))] if n_sems else []) + list(scratch),
        compiler_params=pltpu.CompilerParams(vmem_limit_bytes=vmem << 20),
        cost_estimate=pl.CostEstimate(flops=int(us * 1.1e9), bytes_accessed=0, transcendentals=0),
    )(*[a for _, a in ins])


def side_a(v, axis):
    return lax.ppermute(v, (axis, "c"), SIDE_A)


def side_b(v, axis):
    return lax.ppermute(v, (axis, "c"), SIDE_B)


def side_y(v):
    return lax.ppermute(v, "yl", SWAP)


def core(v):
    return lax.ppermute(v, "c", SWAP)


def ring_gather(own, axis):
    a = side_a(own, axis)
    b = side_b(own, axis)
    return [own, a, b, side_b(a, axis)]


def ring_scatter(parts, axis):
    own, a, b, f = parts
    got = side_b(f, axis)
    other = side_b(b, axis)
    passed = a + got
    return [own, other, side_a(passed, axis)], passed


def chip_gather(own):
    y = side_y(own)
    row = ring_gather(own, "x")
    return row + [y, side_a(y, "x"), side_b(y, "x"), side_y(row[3])]


def norm_parts(v):
    center = v - jnp.mean(v, axis=-1, keepdims=True)
    inv = lax.rsqrt(jnp.mean(center * center, axis=-1, keepdims=True) + EPS)
    return center * inv, inv


def norm_back(vhat, inv, grad, gain):
    t = grad * gain
    return inv * (
        t
        - jnp.mean(t, axis=-1, keepdims=True)
        - vhat * jnp.mean(t * vhat, axis=-1, keepdims=True)
    )


def first_norm(ins, outs, scr, export):
    x, gains = (v.ready() for v in ins)
    vhat, _ = norm_parts(x[...].astype(F32))
    outs[0][...] = (vhat * gains[0:1, :]).astype(BF16)


def stack(*arrays):
    rows = [v.shape[0] for v in arrays]

    def body(ins, outs, scr, export):
        at = 0
        for ref, n in zip(ins, rows):
            outs[0][at : at + n] = ref[...]
            at += n

    return call(body, 1, [("V", v) for v in arrays], [("V", (sum(rows), D), BF16)])[0]


def pack(ins, outs, scr, export):
    at = [0, 0]
    for i, ref in enumerate(ins):
        o = 0 if i < 3 else 1
        export(ref, outs[o].at[pl.ds(at[o], ref.shape[0])])
        at[o] += ref.shape[0]


def own_places(parity, rows):
    i = lax.broadcasted_iota(jnp.int32, (rows, T), 0)
    return ((i // T) * 2 + parity) * T + i % T


def row_of(ends_ref, places):
    row = jnp.zeros_like(places)
    start = jnp.zeros_like(places)
    end = jnp.int32(0)
    for k in range(8):
        end = end + ends_ref[0, k]
        inside = places >= end
        row = row + jnp.where(inside, 1, 0)
        start = jnp.where(inside, end, start)
    return row, places - start


def tables(ins, outs, scr, export):
    idx_ref, len_ref, freq_ref = ins
    turn, mask_out, turn_keep = outs
    c = idx_ref[0]
    n = OWN // 4
    lane = lax.broadcasted_iota(jnp.int32, (n, T), 1)
    token = lax.broadcasted_iota(jnp.int32, (n, T), 0) + (lane // 32) * n
    _, pos = row_of(len_ref, ((token // T) * 2 + c) * T + token % T)
    angle = pos.astype(F32) * freq_ref[...]
    for i, v in enumerate((jnp.cos(angle), jnp.sin(angle))):
        for g in range(4):
            w = jnp.where(lane // 32 == g, v, 0.0)
            w = w + pltpu.roll(w, 32, 1)
            w = w + pltpu.roll(w, 64, 1)
            if i == 1:
                w = jnp.where(lane % 64 < 32, -w, w)
            turn[i, n * g : n * g + n] = w
    export(turn, turn_keep)
    lane = lax.broadcasted_iota(jnp.int32, (OWN, T), 1)
    row, _ = row_of(len_ref, own_places(c, OWN))
    mask_out.ref[0] = jnp.where((lane < 8) & (lane != row), NEG, 0.0).astype(BF16)
    mask_out.ref[1] = jnp.where(lane == row, 1.0, 0.0).astype(BF16)
    row, _ = row_of(len_ref, own_places(1 - c, OWN))
    mask_out.ref[2] = jnp.where(lane == row, 1.0, 0.0).astype(BF16)


def swap_halves(w):
    lane = lax.broadcasted_iota(jnp.int32, w.shape, 1)
    return jnp.where(lane % 64 < 32, pltpu.roll(w, 96, 1), pltpu.roll(w, 32, 1))


def pair_rows(c, own, other):
    first = jnp.where(c == 0, own, other)
    second = jnp.where(c == 0, other, own)
    return jnp.concatenate([first, second], 0)


def block_place(idx_ref, r):
    yl = idx_ref[1] if r < 4 else 1 - idx_ref[1]
    return yl * 4 + idx_ref[2 + r % 4]


def qkv(ins, outs, scr, export):
    idx_ref, own_ref, other_ref, turn = ins[:4]
    blocks = ins[4:]
    q_ref, kv_ref, w_out = outs
    c = idx_ref[0]
    w = jnp.concatenate(
        [
            pair_rows(c, own_ref[64 * i : 64 * i + 64], other_ref[64 * i : 64 * i + 64])
            for i in range(3)
        ],
        0,
    )
    w_out.ref[...] = w
    w_out.flush()
    for half in (0, 4):
        out = mm(jnp.concatenate([v[...] for v in blocks[half : half + 4]], 0), w, NT)
        for i in range(4):
            rows = pl.ds(pl.multiple_of(block_place(idx_ref, half + i) * T, T), T)
            part = out[T * i : T * i + T]
            cos, sin = turn[0, rows, :], turn[1, rows, :]
            q, k = part[:, :T], part[:, T : 2 * T]
            q_ref[rows, :] = ((q * cos + swap_halves(q) * sin) * 0.125).astype(BF16)
            kv_ref[rows, :T] = (k * cos + swap_halves(k) * sin).astype(BF16)
            kv_ref[rows, T:] = part[:, 2 * T :].astype(BF16)


Q = 256


def head_lanes(w):
    lane = lax.broadcasted_iota(jnp.int32, w.shape, 1)
    fill = jnp.zeros_like(w)
    return jnp.where(lane < 64, w, fill), jnp.where(lane < 64, fill, w)


def diag_masks(c, queries_first):
    shape = (Q, Q)
    i = lax.broadcasted_iota(jnp.int32, shape, 0 if queries_first else 1)
    k = lax.broadcasted_iota(jnp.int32, shape, 1 if queries_first else 0)
    own = k <= i
    kb, ib = k // T, i // T
    other = (kb < ib) | ((kb == ib) & (c == 1))
    return own, other


def turned(w):
    return w.astype(F32).T.astype(BF16)


def attend(ins, outs, scr, export):
    idx_ref, q_ref, kv_ref, kvo_ref, mask = ins[:5]
    o_ref, o_keep, lse, q_keep, kv_keep, kvo_keep, n_keep = outs
    (vt,) = scr
    export(q_ref, q_keep)
    export(kv_ref, kv_keep)
    export(kvo_ref, kvo_keep)
    for r in range(8):
        export(ins[5 + r], n_keep.at[pl.ds(pl.multiple_of(block_place(idx_ref, r) * T, T), T)])
    for i, kv in enumerate((kv_ref, kvo_ref)):
        for b in range(OWN // Q):
            vt[i, :, Q * b : Q * b + Q] = turned(kv[Q * b : Q * b + Q, T:])
    mask = mask.ready()
    masks = diag_masks(idx_ref[0], False)
    ones = jnp.ones((16, 2 * Q), BF16)

    def query_tile(jt, carry):
        first = pl.multiple_of(jt * Q, Q)
        qrows = pl.ds(first, Q)
        mq = mask[0, qrows, :]
        qa = [jnp.concatenate([h, mq], 1) for h in head_lanes(q_ref[qrows, :])]

        def tile(it, state, diag):
            rows = pl.ds(pl.multiple_of(it * Q, Q), Q)
            v = jnp.concatenate([vt[0, :, rows], vt[1, :, rows]], 1)
            k = [
                jnp.concatenate([kv[rows, :T], mask[1 + i, rows, :]], 1)
                for i, kv in enumerate((kv_ref, kvo_ref))
            ]
            out = []
            for h in range(2):
                m, acc = state[h]
                s = [mm(k[i], qa[h], NT) for i in range(2)]
                if diag:
                    s = [jnp.where(masks[i], s[i], NEG) for i in range(2)]
                top = jnp.max(jnp.maximum(s[0], s[1]), axis=0, keepdims=True)
                m_new = jnp.maximum(m, top)
                p = jnp.concatenate([jnp.exp(v_ - m_new).astype(BF16) for v_ in s], 0)
                vh = jnp.concatenate([v[64 * h : 64 * h + 64], ones], 0)
                out.append((m_new, acc * jnp.exp(m - m_new) + mm(vh, p)))
            return tuple(out)

        zero = (jnp.full((1, Q), NEG, F32), jnp.zeros((80, Q), F32))
        state = tile(jt, (zero, zero), True)
        state = lax.fori_loop(0, jt, lambda it, st: tile(it, st, False), state)
        o = jnp.concatenate([acc[:64] / acc[64:65] for _, acc in state], 0)
        o_keep.ref[:, qrows] = o
        o = o.T.astype(BF16)
        for b in range(Q // T):
            o_ref[jt * (Q // T) + b] = o[b * T : b * T + T]
        for h, (m, acc) in enumerate(state):
            lse.ref[pl.ds(h, 1), qrows] = m + jnp.log(acc[64:65])
        return carry

    lax.fori_loop(0, OWN // Q, query_tile, 0)


DOUBLED = [0, 4, 1, 5, 2, 6, 3, 7]


def middle(ins, outs, scr, export):
    idx_ref, o_ref, own_ref, other_ref, x_l, gains_l = ins
    n2_ref, stat_ref, a_out, h_out, o_out, w_out = outs
    c = idx_ref[0]
    o = jnp.concatenate([o_ref[j] for j in range(8)], 1)
    o_out.ref[...] = o
    o_out.flush()
    for i, r in enumerate(DOUBLED):
        rows = pl.ds(pl.multiple_of(block_place(idx_ref, r) * T, T), T)
        j = DOUBLED.index(r ^ 3 if r % 4 in (1, 2) else r)
        part, part_o = slice(64 * i, 64 * i + 64), slice(64 * j, 64 * j + 64)
        w_out.ref[rows, :] = pair_rows(c, own_ref[part], other_ref[part_o])
    w_out.flush()
    a = mm(o, w_out.ref[...])
    a_out.ref[...] = a
    a_out.flush()
    vhat, _ = norm_parts(a)
    x_ref, gains_ref = x_l.ready(), gains_l.ready()
    h = x_ref[...].astype(F32) + vhat * gains_ref[1:2, :]
    h_out.ref[...] = h
    h_out.flush()
    vhat, _ = norm_parts(h)
    n2_ref[...] = (vhat * gains_ref[2:3, :]).astype(BF16)
    stat_ref[...] = jnp.zeros((8, T), F32) + jnp.sum(a * a) * (1.0 / D)


def gelu_tanh(u):
    return jnp.tanh(GELU_A * (u + GELU_B * u * u * u))


def mlp_forward(ins, outs, scr, export):
    ns, ws = ins[:4], ins[4:8]
    u_ref, n_out, parts = outs[0], outs[1], outs[2:]
    for i, ref in enumerate(ns):
        export(ref, n_out.at[pl.ds(T * i, T)])
    n = jnp.concatenate([r[...] for r in ns], 0)
    m = None
    for s in range(4):
        w = ws[s].ready()
        u = mm(n, w[:256], NT)
        u_ref[:, 256 * s : 256 * s + 256] = u
        z = (0.5 * u * (1.0 + gelu_tanh(u))).astype(BF16)
        part = mm(z, w[256:])
        m = part if m is None else m + part
    for i in range(4):
        parts[i][...] = m[T * i : T * i + T].astype(BF16)


def total_of(refs):
    total = refs[0][...].astype(F32)
    for ref in refs[1:]:
        total = total + ref[...].astype(F32)
    return total


def turn_back(ins, outs, scr, export):
    h_ref, gains_ref, up_ref = (v.ready() for v in ins[3:])
    out_ref, g_ref, dc_ref, stat_ref = outs
    m = total_of(ins[:3])
    vhat, inv = norm_parts(m)
    gain = gains_ref[3:4, :]
    dy = up_ref[...].astype(F32)
    g_ref[...] = norm_back(vhat, inv, dy, gain).astype(BF16)
    dc_ref[...] = jnp.sum(dy * vhat, axis=0, keepdims=True)
    stat_ref[...] = jnp.zeros((8, T), F32) + jnp.sum(m * m) * (1.0 / D)
    out_ref[...] = (h_ref[...] + vhat * gain).astype(BF16)


def mlp_backward(ins, outs, scr, export):
    gs, ws, u_ref = ins[:4], ins[4:8], ins[8]
    z_ref, du_ref, parts = outs[0], outs[1], outs[2:]
    g = jnp.concatenate([r[...] for r in gs], 0)
    dn = None
    for s in range(4):
        cols = slice(256 * s, 256 * s + 256)
        u = u_ref[:, cols]
        t = gelu_tanh(u)
        z_ref[:, cols] = (0.5 * u * (1.0 + t)).astype(BF16)
        slope = 0.5 * (1.0 + t) + 0.5 * u * (1.0 - t * t) * GELU_A * (1.0 + 3.0 * GELU_B * u * u)
        w = ws[s].ready()
        du = (mm(g, w[256:], NT) * slope).astype(BF16)
        du_ref[:, cols] = du
        part = mm(du, w[:256])
        dn = part if dn is None else dn + part
    for i in range(4):
        parts[i][...] = dn[T * i : T * i + T].astype(BF16)


def mlp_grads(ins, outs, scr, export):
    n_l, z, du, gs = ins[0], ins[1], ins[2], ins[3:]
    send_ref, keep = outs
    g = jnp.concatenate([r[...] for r in gs], 0)
    n = n_l.ready()[...]
    for s, ref, slot in ((1, send_ref, 0), (3, send_ref, 1), (0, keep.ref, 0), (2, keep.ref, 1)):
        cols = slice(256 * s, 256 * s + 256)
        ref[slot, :256] = mm(du[:, cols], n, TN).astype(BF16)
        ref[slot, 256:] = mm(z[:, cols], g, TN).astype(BF16)


def back_middle(ins, outs, scr, export):
    h_ref, a_ref, gains_l, up_l, wo_ref = ins[3:]
    gains_ref, up_ref = gains_l.ready(), up_l.ready()
    do_ref, dc_ref, dh_out, ga_out = outs
    dn = total_of(ins[:3])
    vhat, inv = norm_parts(h_ref.ready()[...])
    dc_ref[1:2, :] = jnp.sum(dn * vhat, axis=0, keepdims=True)
    dh = up_ref[...].astype(F32) + norm_back(vhat, inv, dn, gains_ref[2:3, :])
    dh_out.ref[...] = dh
    dh_out.flush()
    vhat, inv = norm_parts(a_ref.ready()[...])
    dc_ref[0:1, :] = jnp.sum(dh * vhat, axis=0, keepdims=True)
    ga = norm_back(vhat, inv, dh, gains_ref[1:2, :]).astype(BF16)
    ga_out.ref[...] = ga
    ga_out.flush()
    do = mm(ga, wo_ref.ready()[...], NT).astype(BF16)
    for j in range(8):
        do_ref[j] = do[:, T * j : T * j + T]


def attend_back(ins, outs, scr, export):
    idx_ref = ins[0]
    do_ref, q_ref, kv_ref, kvo_ref, o_ref, mask, lse, tab = ins[1:]
    dq_out, oth_out, own_out = outs
    acco, kt = scr
    own_ref = own_out.ref
    kv_ref, kvo_ref, mask = kv_ref.ready(), kvo_ref.ready(), mask.ready()
    for i, kv in enumerate((kv_ref, kvo_ref)):
        for b in range(OWN // Q):
            kt[i, :, Q * b : Q * b + Q] = turned(kv[Q * b : Q * b + Q, :T])
    own_ref[...] = jnp.zeros_like(own_ref)
    acco[...] = jnp.zeros_like(acco)
    masks = diag_masks(idx_ref[0], False)
    do_ref, q_ref, o_ref, lse, tab = (v.ready() for v in (do_ref, q_ref, o_ref, lse, tab))

    def query_tile(jt, carry):
        qrows = pl.ds(pl.multiple_of(jt * Q, Q), Q)
        do = do_ref[qrows, :]
        q_h, do_h = head_lanes(q_ref[qrows, :]), head_lanes(do)
        mq = mask[0, qrows, :]
        qa = [jnp.concatenate([h, mq], 1) for h in q_h]
        inner = do.astype(F32).T * o_ref[:, qrows]
        delta = [jnp.sum(inner[64 * h : 64 * h + 64], axis=0, keepdims=True) for h in range(2)]
        top = [lse[pl.ds(h, 1), qrows] for h in range(2)]
        q_st, do_st = jnp.concatenate(q_h, 0), jnp.concatenate(do_h, 0)

        def tile(it, dq, diag):
            rows = pl.ds(pl.multiple_of(it * Q, Q), Q)
            dq = list(dq)
            for i, (kv, acc) in enumerate(((kv_ref, own_ref), (kvo_ref, acco))):
                ka = jnp.concatenate([kv[rows, :T], mask[1 + i, rows, :]], 1)
                v = kv[rows, T:]
                ps, ss = [], []
                for h in range(2):
                    p = jnp.exp(mm(ka, qa[h], NT) - top[h])
                    if diag:
                        p = jnp.where(masks[i], p, 0.0)
                    s = (p * (mm(v, do_h[h], NT) - delta[h])).astype(BF16)
                    ps.append(p.astype(BF16))
                    ss.append(s)
                    dq[h] = dq[h] + mm(kt[i, 64 * h : 64 * h + 64, rows], s)
                acc[rows, :T] += mm(jnp.concatenate(ss, 1), q_st)
                acc[rows, T:] += mm(jnp.concatenate(ps, 1), do_st)
            return tuple(dq)

        zero = jnp.zeros((64, Q), F32)
        dq = tile(jt, (zero, zero), True)
        dq = lax.fori_loop(0, jt, lambda it, st: tile(it, st, False), dq)
        dq = jnp.concatenate(dq, 0).T * 0.125
        dq_out.ref[qrows, :] = (
            dq * tab[0, qrows, :] + swap_halves(dq * tab[1, qrows, :])
        ).astype(BF16)
        return carry

    lax.fori_loop(0, OWN // Q, query_tile, 0)
    own_out.flush()
    dq_out.flush()
    oth_out.ref[...] = acco[...].astype(BF16)


def input_back(ins, outs, scr, export):
    idx_ref = ins[0]
    dq_ref, own_ref, recv_ref, w_l, turn_l = ins[1:]
    dq_ref, own_ref, recv_ref = dq_ref.ready(), own_ref.ready(), recv_ref.ready()
    g_ref = scr[0]
    g_out, parts = outs[0], outs[1:]
    tab = turn_l.ready()
    both = own_ref[...] + recv_ref[...].astype(F32)
    dk = both[:, :T]
    g_ref[:, :T] = dq_ref[...]
    g_ref[:, T : 2 * T] = (dk * tab[0] + swap_halves(dk * tab[1])).astype(BF16)
    g_ref[:, 2 * T :] = both[:, T:].astype(BF16)
    export(g_ref, g_out)
    w = w_l.ready()[...]
    for half in (4, 0):
        rows = [
            pl.ds(pl.multiple_of(block_place(idx_ref, r) * T, T), T)
            for r in DOUBLED[half : half + 4]
        ]
        out = mm(jnp.concatenate([g_ref[r, :] for r in rows], 0), w)
        parts[half // 4][...] = out.astype(BF16)


def attn_grads(ins, outs, scr, export):
    idx_ref, g_l, n_l, w_l, gains_l, dc12_ref, dc3_ref, stat_a, stat_m = ins
    gains_ref = gains_l.ready()
    send_ref, own_ref = outs
    c = idx_ref[0]
    g, n, w_ref = g_l.ready(), n_l.ready(), w_l.ready()
    dc = jnp.zeros((1, D), F32)
    for i in range(3):
        w = mm(g[:, T * i : T * i + T], n[...], TN)
        dc = dc + jnp.sum(w * w_ref[T * i : T * i + T, :].astype(F32), axis=0, keepdims=True)
        own_ref[64 * i : 64 * i + 64] = jnp.where(c == 0, w[:64], w[64:]).astype(BF16)
        send_ref[64 * i : 64 * i + 64] = jnp.where(c == 0, w[64:], w[:64]).astype(BF16)
    row = lax.broadcasted_iota(jnp.int32, (16, D), 0)
    strip = jnp.zeros((16, D), F32)
    extra = [dc / gains_ref[0:1, :], dc12_ref[0:1, :], dc12_ref[1:2, :], dc3_ref[...]]
    extra += [stat_a[0:1, 0:1], stat_m[0:1, 0:1]]
    for i, v in enumerate(extra):
        strip = jnp.where(row == i, v, strip)
    own_ref[192:] = strip.astype(BF16)
    send_ref[192:] = strip.astype(BF16)


def proj_grads(ins, outs, scr, export):
    idx_ref, o_l, ga_l = ins
    c = idx_ref[0]
    oth, own = outs
    w = scr[0]
    w[...] = mm(o_l.ready()[...], ga_l.ready()[...], TN)
    for i, r in enumerate(DOUBLED):
        base = block_place(idx_ref, r) * T
        mine = pl.ds(pl.multiple_of(base + c * 64, 64), 64)
        other = pl.ds(pl.multiple_of(base + (1 - c) * 64, 64), 64)
        j = DOUBLED.index(r ^ 3 if r % 4 in (1, 2) else r)
        own.ref[64 * i : 64 * i + 64] = w[mine, :].astype(BF16)
        oth[64 * j : 64 * j + 64] = w[other, :].astype(BF16)


def fold(ins, outs, scr, export):
    a, b = ins
    a = a.ready() if isinstance(a, Load) else a
    n = outs[0].shape[0]
    outs[0][...] = a[:n] + b[:n]
    outs[1][...] = a[n:] + b[n:]


def last(ins, outs, scr, export):
    x_ref, dh_l, gains_ref = (v.ready() for v in ins[2:])
    vhat, inv = norm_parts(x_ref[...].astype(F32))
    outs[0][...] = dh_l[...] + norm_back(vhat, inv, total_of(ins[:2]), gains_ref[0:1, :])


def halves_sum(ins, outs, scr, export):
    keep, got = ins[0].ready(), ins[1]
    outs[0].ref[...] = keep[0] + got[0]
    other = keep[1] + got[1]
    outs[1][...] = other[:256]
    outs[2][...] = other[256:]


def ring_blocks(idx_ref, whole, outs, n, extra=None):
    at = lambda i: pl.ds(pl.multiple_of(idx_ref[6 + i] * n, n), n)
    m = n if extra is None else n + extra.shape[0]
    for i, (ref, first) in enumerate(((outs[0], 0), (outs[1], 0), (outs[2], 0), (outs[2], m))):
        ref[first : first + n] = whole[at(i), :]
        if extra is not None:
            ref[first + n : first + m] = extra


def mlp_blocks(ins, outs, scr, export):
    idx_ref, mine, inner, outer = ins
    mine = mine.ready()
    scr[0][:256] = mine[:256] + inner[...]
    scr[0][256:] = mine[256:] + outer[...]
    ring_blocks(idx_ref, scr[0], outs, 128)


def attn_blocks(ins, outs, scr, export):
    idx_ref, own, got, *proj = ins
    scr[0][:192] = own[:192] + got[:192]
    scr[0][192:] = total_of(proj).astype(BF16)
    ring_blocks(idx_ref, scr[0], outs, 64, own[192:] + got[192:])


def spread(ins, outs, scr, export):
    idx_ref = ins[0]
    n = scr[0].shape[1]
    for r in range(4):
        scr[0][idx_ref[6 + r]] = ins[1 + r][:n].astype(F32)
    rows = 0
    for ref in outs:
        for i in range(ref.shape[0] // n):
            export(scr[0].at[rows], ref.at[pl.ds(i * n, n)])
            rows += 1


def data_sum(idx, own, a, got, n, shapes):
    m = own.shape[0]
    mine = own + got[:m] + side_a(a + got[m:], "z")
    mine = mine + lax.ppermute(mine, "yh", SWAP)
    return mine, call(
        spread,
        1,
        [("S", idx)] + [("V", v) for v in ring_gather(mine, "z")],
        [("X", s, F32) for s in shapes],
        scratch=[pltpu.VMEM((4, n, D), F32)],
        exports=4,
    )


def after(values, event):
    return lax.optimization_barrier((*values, event))[: len(values)]


def on_device(x, lengths, gains, wq, wk, wv, wo, wup, wdown, upstream):
    c, yl, xi, z = (lax.axis_index(n) for n in ("c", "yl", "x", "z"))

    def ring(i):
        first, second = i ^ 1, (i + 2 * (i & 1) + 3) & 3
        return [i, jnp.where(c == 0, first, second), jnp.where(c == 0, second, first), i ^ 2]

    idx = jnp.stack([c, yl, *ring(xi), *ring(z)]).astype(jnp.int32)
    freq = (10000.0 ** (-2.0 * np.arange(32) / 64.0)).astype(np.float32)
    freq = jnp.asarray(np.tile(freq, 4)[None, :])
    bf = lambda k, *s: (k, s, BF16)
    f32 = lambda k, *s: (k, s, F32)
    many = lambda k, arrays: [(k, a) for a in arrays]
    I = ("S", idx)
    G, X, U = ("H", gains), ("H", x), ("H", upstream)

    (n1,) = call(first_norm, 1, [X, G], [bf("V", T, D)])
    n1 = chip_gather(n1)
    wqkv, w_own = call(
        pack, 1, many("R", (wq, wk, wv, wup, wdown)), [bf("V", 192, D), bf("X", 512, D)], exports=5
    )
    wqkv_o = core(wqkv)
    w_core = core(w_own)
    w_y = lax.ppermute(w_own, ("yh", "yl"), OUTER)
    wo_all = stack(wo, side_y(wo))
    wo_all = stack(wo_all, side_a(wo_all, "x"))
    wo_all = stack(wo_all, side_b(wo_all, "x"))
    turn, mask, turn_keep = call(
        tables,
        2,
        [I, ("S", lengths), ("V", freq)],
        [f32("V", 2, OWN, T), bf("H", 3, OWN, T), f32("X", 2, OWN, T)],
        exports=1,
    )
    q, kv, w_pair = call(
        qkv,
        3,
        [I, ("V", wqkv), ("V", wqkv_o), ("V", turn)] + many("V", n1),
        [bf("V", OWN, T), bf("V", OWN, 2 * T), bf("H", 3 * T, D)],
    )
    kvo = core(kv)
    q, w_core, w_y, wo_all = after([q, w_core, w_y, wo_all], kvo)
    wo_c = core(wo_all)
    o, o32, lse, q_keep, kv_keep, kvo_keep, n1_all = call(
        attend,
        10,
        [I, ("V", q), ("V", kv), ("V", kvo), ("H", mask)] + many("V", n1),
        [
            bf("V", 8, T, T),
            f32("H", T, OWN),
            f32("H", 8, OWN),
            bf("X", OWN, T),
            bf("X", OWN, 2 * T),
            bf("X", OWN, 2 * T),
            bf("X", OWN, D),
        ],
        scratch=[pltpu.VMEM((2, T, OWN), BF16)],
        exports=11,
    )
    o_all = lax.all_to_all(o, ("yl", "x"), 0, 0, tiled=True)
    n2, stat_a, a, h, o_full, wo_full = call(
        middle,
        2,
        [I, ("V", o_all), ("V", wo_all), ("V", wo_c), X, G],
        [bf("V", T, D), f32("V", 8, T), f32("H", T, D), f32("H", T, D), bf("H", T, D), bf("H", D, D)],
    )
    (w_y,) = after([w_y], n2)
    ws = many("H", (w_own, w_core, w_y, core(w_y)))
    u, n2_all, *parts = call(
        mlp_forward,
        4,
        many("V", ring_gather(n2, "x")) + ws,
        [f32("V", 4 * T, D), bf("X", 4 * T, D)] + [bf("V", T, D)] * 4,
        vmem=24,
        exports=4,
    )
    terms, _ = ring_scatter(parts, "x")
    block_out, gm, dc3, stat_m = call(
        turn_back,
        1,
        many("V", terms) + [("H", h), G, U],
        [bf("V", T, D), bf("V", T, D), f32("V", 1, D), f32("V", 8, T)],
    )
    gm = ring_gather(gm, "x")
    zz, du, *parts = call(
        mlp_backward,
        4,
        many("V", gm) + ws + [("V", u)],
        [bf("V", 4 * T, D), bf("V", 4 * T, D)] + [bf("V", T, D)] * 4,
        vmem=24,
    )
    terms, passed = ring_scatter(parts, "x")
    zz, du = after([zz, du], passed)
    send, keep = call(
        mlp_grads,
        30,
        [("H", n2_all), ("V", zz), ("V", du)] + many("V", gm),
        [bf("V", 2, 512, D), bf("H", 2, 512, D)],
    )
    got = core(send)
    do, dc12, dh, ga = call(
        back_middle,
        30,
        many("V", terms) + [("H", h), ("H", a), G, U, ("H", wo_full)],
        [bf("V", 8, T, T), f32("V", 2, D), f32("H", T, D), bf("H", T, D)],
    )
    mine, oa, ob = call(
        halves_sum, 1, [("H", keep), ("V", got)], [bf("H", 512, D), bf("V", 256, D), bf("V", 256, D)]
    )
    inner = side_y(oa)
    outer = lax.ppermute(ob, ("yh", "yl"), OUTER)
    (do,) = after([do], oa)
    do_all = lax.all_to_all(do, ("yl", "x"), 0, 0, tiled=True).reshape(OWN, T)
    po_send, po = call(
        proj_grads,
        2,
        [I, ("H", o_full), ("H", ga)],
        [bf("V", 512, D), bf("H", 512, D)],
        scratch=[pltpu.VMEM((D, D), F32)],
    )
    po_got = core(po_send)
    po, po_send = call(fold, 1, [("H", po), ("V", po_got)], [bf("V", 256, D)] * 2)
    m_blocks = call(
        mlp_blocks,
        1,
        [I, ("H", mine), ("V", inner), ("V", outer)],
        [bf("V", 128, D), bf("V", 128, D), bf("V", 256, D)],
        scratch=[pltpu.VMEM((512, D), BF16)],
    )
    got_z = side_b(m_blocks[2], "z")
    (do_all,) = after([do_all], (m_blocks[2], po_send))
    po_got = side_b(po_send, "x")
    dq, oth, own32 = call(
        attend_back,
        140,
        [I] + many("H", (do_all, q_keep, kv_keep, kvo_keep, o32, mask, lse, turn_keep)),
        [bf("H", OWN, T), bf("H", OWN, 2 * T), f32("H", OWN, 2 * T)],
        scratch=[pltpu.VMEM((OWN, 2 * T), F32), pltpu.VMEM((2, T, OWN), BF16)],
        vmem=60,
    )
    recv = core(oth)
    dqkv, part, part_send = call(
        input_back,
        2,
        [I] + many("H", (dq, own32, recv, w_pair, turn_keep)),
        [bf("X", OWN, 3 * T), bf("V", 4 * T, D), bf("V", 4 * T, D)],
        scratch=[pltpu.VMEM((OWN, 3 * T), BF16)],
        exports=1,
    )
    part, part_send = call(
        fold, 1, many("V", (part, side_b(part_send, "x"))), [bf("V", 2 * T, D)] * 2
    )
    part, part_send = call(
        fold, 1, many("V", (part, side_a(part_send, "x"))), [bf("V", T, D)] * 2
    )
    g_send, g_own = call(
        attn_grads,
        2,
        [I, ("H", dqkv), ("H", n1_all), ("H", w_pair), G] + many("V", (dc12, dc3, stat_a, stat_m)),
        [bf("V", 208, D), bf("V", 208, D)],
    )
    g_recv = core(g_send)
    (input_grad,) = call(
        last, 1, many("V", (part, side_y(part_send))) + [X, ("H", dh), G], [f32("V", T, D)]
    )
    _, (g_up, g_down) = data_sum(idx, m_blocks[0], m_blocks[1], got_z, 128, [(256, D), (256, D)])

    po, po_send = call(fold, 1, many("V", (po, po_got)), [bf("V", 128, D)] * 2)
    po, po_send = call(fold, 1, many("V", (po, side_a(po_send, "x"))), [bf("V", 64, D)] * 2)
    blocks = call(
        attn_blocks,
        1,
        [I] + many("V", (g_own, g_recv, po, side_y(po_send))),
        [bf("V", 80, D), bf("V", 80, D), bf("V", 160, D)],
        scratch=[pltpu.VMEM((256, D), BF16)],
    )
    mine, (g_q, g_k, g_v, g_o) = data_sum(
        idx, blocks[0], blocks[1], side_b(blocks[2], "z"), 64, [(64, D)] * 4
    )

    rows = mine[64:72].astype(F32)
    rows = rows + side_a(rows, "x")
    rows = rows + side_b(rows, "x")
    rows = rows + side_y(rows)
    stats = rows[4:6, 0] * (1.0 / 16384.0)
    return block_out, input_grad, g_q, g_k, g_v, g_o, g_up, g_down, rows[:4], stats


def solution(mesh):
    names = ("yh", "z", "yl", "x", "c")
    fine = Mesh(np.asarray(mesh.devices).reshape(2, 4, 2, 4, 2), names)
    tokens, group, shard = P(names, None), P(("yh", "z"), None), P(("yl", "x", "c"), None)
    return jax.shard_map(
        on_device,
        mesh=fine,
        in_specs=(tokens, group, P(), shard, shard, shard, shard, shard, shard, tokens),
        out_specs=(tokens, tokens, shard, shard, shard, shard, shard, shard, P(), P()),
        check_vma=False,
    )
```

```python
import functools

import jax
import jax.numpy as jnp
import numpy as np
from jax import lax
from jax.experimental import pallas as pl
from jax.experimental.pallas import tpu as pltpu
from jax.sharding import Mesh
from jax.sharding import PartitionSpec as P

D = 1024
T = 128
NB = 8
OWN = NB * T
F32 = jnp.float32
BF16 = jnp.bfloat16
NEG = -1e30
EPS = 1e-05
MATCH = ([(0, 1), (1, 0), (2, 3), (3, 2)], [(1, 2), (2, 1), (3, 0), (0, 3)])
SIDE_A = [(2 * i + c, 2 * j + c) for c in range(2) for i, j in MATCH[c]]
SIDE_B = [(2 * i + c, 2 * j + c) for c in range(2) for i, j in MATCH[1 - c]]
SWAP = [(0, 1), (1, 0)]
OUTER = [(0, 3), (3, 0), (1, 2), (2, 1)]
NT = (((1,), (1,)), ((), ()))
NN = (((1,), (0,)), ((), ()))
TN = (((0,), (0,)), ((), ()))
GELU_A = float(np.sqrt(2.0 / np.pi))
GELU_B = 0.044715


def mm(a, b, dims=NN):
    return lax.dot_general(a, b, dims, preferred_element_type=F32)


class Load:
    def __init__(self, src, dst, sem):
        self.copy, self.dst, self.waited = pltpu.make_async_copy(src, dst, sem), dst, False
        self.copy.start()

    def ready(self):
        if not self.waited:
            self.copy.wait()
            self.waited = True
        return self.dst


class Store:
    def __init__(self, src, dst, sem):
        self.copy, self.ref, self.sent = pltpu.make_async_copy(src, dst, sem), src, False

    def flush(self):
        if not self.sent:
            self.copy.start()
            self.sent = True


def call(body, us, ins, outs, vmem=16, scratch=(), exports=0):
    space = {"S": pltpu.SMEM, "V": pltpu.VMEM, "H": pltpu.HBM, "X": pltpu.HBM, "R": pltpu.HBM}
    kinds_in, kinds_out = [k for k, _ in ins], [k for k, _, _ in outs]
    buffers = [pltpu.VMEM(a.shape, a.dtype) for k, a in ins if k == "H"]
    buffers += [pltpu.VMEM(s, d) for k, s, d in outs if k == "H"]
    n_sems = len(buffers) + exports

    def kernel(*refs):
        refs = list(refs)
        n_in, n_out = len(ins), len(outs)
        raw_in, raw_out = refs[:n_in], refs[n_in : n_in + n_out]
        held = refs[n_in + n_out : n_in + n_out + len(buffers)]
        rest = refs[n_in + n_out + len(buffers) :]
        if n_sems:
            sems, rest = rest[0], rest[1:]
        used = [0]
        exported = []

        def sem():
            used[0] += 1
            return sems.at[used[0] - 1]

        def export(src, dst):
            copy = pltpu.make_async_copy(src, dst, sem())
            copy.start()
            exported.append(copy)

        held = list(held)
        loads = [Load(r, held.pop(0), sem()) if k == "H" else r for k, r in zip(kinds_in, raw_in)]
        stores = [Store(held.pop(0), r, sem()) if k == "H" else r for k, r in zip(kinds_out, raw_out)]
        body(loads, stores, rest, export)
        for s in stores:
            if isinstance(s, Store):
                s.flush()
        for v in loads:
            if isinstance(v, Load):
                v.ready()
        for s in stores:
            if isinstance(s, Store):
                s.copy.wait()
        for copy in exported:
            copy.wait()

    return pl.pallas_call(
        kernel,
        out_shape=tuple(jax.ShapeDtypeStruct(s, d) for _, s, d in outs),
        in_specs=[pl.BlockSpec(memory_space=space[k]) for k in kinds_in],
        out_specs=tuple(pl.BlockSpec(memory_space=space[k]) for k in kinds_out),
        scratch_shapes=buffers + ([pltpu.SemaphoreType.DMA((n_sems,))] if n_sems else []) + list(scratch),
        compiler_params=pltpu.CompilerParams(vmem_limit_bytes=vmem << 20),
        cost_estimate=pl.CostEstimate(flops=int(us * 1.1e9), bytes_accessed=0, transcendentals=0),
    )(*[a for _, a in ins])


def side_a(v, axis):
    return lax.ppermute(v, (axis, "c"), SIDE_A)


def side_b(v, axis):
    return lax.ppermute(v, (axis, "c"), SIDE_B)


def side_y(v):
    return lax.ppermute(v, "yl", SWAP)


def core(v):
    return lax.ppermute(v, "c", SWAP)


def ring_gather(own, axis):
    a = side_a(own, axis)
    b = side_b(own, axis)
    return [own, a, b, side_b(a, axis)]


def ring_scatter(parts, axis):
    own, a, b, f = parts
    got = side_b(f, axis)
    other = side_b(b, axis)
    passed = a + got
    return [own, other, side_a(passed, axis)], passed


def chip_gather(own):
    y = side_y(own)
    row = ring_gather(own, "x")
    return row + [y, side_a(y, "x"), side_b(y, "x"), side_y(row[3])]


def norm_parts(v):
    center = v - jnp.mean(v, axis=-1, keepdims=True)
    inv = lax.rsqrt(jnp.mean(center * center, axis=-1, keepdims=True) + EPS)
    return center * inv, inv


def norm_back(vhat, inv, grad, gain):
    t = grad * gain
    return inv * (
        t
        - jnp.mean(t, axis=-1, keepdims=True)
        - vhat * jnp.mean(t * vhat, axis=-1, keepdims=True)
    )


def first_norm(ins, outs, scr, export):
    x, gains = (v.ready() for v in ins)
    vhat, _ = norm_parts(x[...].astype(F32))
    outs[0].ref[...] = (vhat * gains[0:1, :]).astype(BF16)


def stack(*arrays):
    rows = [v.shape[0] for v in arrays]

    def body(ins, outs, scr, export):
        at = 0
        for ref, n in zip(ins, rows):
            outs[0][at : at + n] = ref[...]
            at += n

    return call(body, 1, [("V", v) for v in arrays], [("V", (sum(rows), D), BF16)])[0]


def pack(ins, outs, scr, export):
    at = [0, 0]
    for i, ref in enumerate(ins):
        o = 0 if i < 3 else 1
        export(ref, outs[o].at[pl.ds(at[o], ref.shape[0])])
        at[o] += ref.shape[0]


def own_places(parity, rows):
    i = lax.broadcasted_iota(jnp.int32, (rows, T), 0)
    return ((i // T) * 2 + parity) * T + i % T


def row_of(ends_ref, places):
    row = jnp.zeros_like(places)
    start = jnp.zeros_like(places)
    end = jnp.int32(0)
    for k in range(8):
        end = end + ends_ref[0, k]
        inside = places >= end
        row = row + jnp.where(inside, 1, 0)
        start = jnp.where(inside, end, start)
    return row, places - start


def tables(ins, outs, scr, export):
    idx_ref, len_ref, freq_ref = ins
    turn, mask_out, turn_keep = outs
    c = idx_ref[0]
    n = OWN // 4
    lane = lax.broadcasted_iota(jnp.int32, (n, T), 1)
    token = lax.broadcasted_iota(jnp.int32, (n, T), 0) + (lane // 32) * n
    _, pos = row_of(len_ref, ((token // T) * 2 + c) * T + token % T)
    angle = pos.astype(F32) * freq_ref[...]
    for i, v in enumerate((jnp.cos(angle), jnp.sin(angle))):
        for g in range(4):
            w = jnp.where(lane // 32 == g, v, 0.0)
            w = w + pltpu.roll(w, 32, 1)
            w = w + pltpu.roll(w, 64, 1)
            if i == 1:
                w = jnp.where(lane % 64 < 32, -w, w)
            turn[i, n * g : n * g + n] = w
    export(turn, turn_keep)
    lane = lax.broadcasted_iota(jnp.int32, (OWN, T), 1)
    row, _ = row_of(len_ref, own_places(c, OWN))
    mask_out.ref[0] = jnp.where((lane < 8) & (lane != row), NEG, 0.0).astype(BF16)
    mask_out.ref[1] = jnp.where(lane == row, 1.0, 0.0).astype(BF16)
    row, _ = row_of(len_ref, own_places(1 - c, OWN))
    mask_out.ref[2] = jnp.where(lane == row, 1.0, 0.0).astype(BF16)


def swap_halves(w):
    lane = lax.broadcasted_iota(jnp.int32, w.shape, 1)
    return jnp.where(lane % 64 < 32, pltpu.roll(w, 96, 1), pltpu.roll(w, 32, 1))


def pair_rows(c, own, other):
    first = jnp.where(c == 0, own, other)
    second = jnp.where(c == 0, other, own)
    return jnp.concatenate([first, second], 0)


def block_place(idx_ref, r):
    yl = idx_ref[1] if r < 4 else 1 - idx_ref[1]
    return yl * 4 + idx_ref[2 + r % 4]


def qkv(ins, outs, scr, export):
    idx_ref, own_ref, other_ref, turn = ins[:4]
    blocks = ins[4:]
    q_ref, kv_ref, w_out = outs
    c = idx_ref[0]
    w = jnp.concatenate(
        [
            pair_rows(c, own_ref[64 * i : 64 * i + 64], other_ref[64 * i : 64 * i + 64])
            for i in range(3)
        ],
        0,
    )
    w_out.ref[...] = w
    w_out.flush()
    for half in (0, 4):
        out = mm(jnp.concatenate([v[...] for v in blocks[half : half + 4]], 0), w, NT)
        for i in range(4):
            rows = pl.ds(pl.multiple_of(block_place(idx_ref, half + i) * T, T), T)
            part = out[T * i : T * i + T]
            cos, sin = turn[0, rows, :], turn[1, rows, :]
            q, k = part[:, :T], part[:, T : 2 * T]
            q_ref[rows, :] = ((q * cos + swap_halves(q) * sin) * 0.125).astype(BF16)
            kv_ref[rows, :T] = (k * cos + swap_halves(k) * sin).astype(BF16)
            kv_ref[rows, T:] = part[:, 2 * T :].astype(BF16)


Q = 256


def head_lanes(w):
    lane = lax.broadcasted_iota(jnp.int32, w.shape, 1)
    fill = jnp.zeros_like(w)
    return jnp.where(lane < 64, w, fill), jnp.where(lane < 64, fill, w)


def diag_masks(c):
    k = lax.broadcasted_iota(jnp.int32, (Q, Q), 0)
    i = lax.broadcasted_iota(jnp.int32, (Q, Q), 1)
    kb, ib = k // T, i // T
    return k <= i, (kb < ib) | ((kb == ib) & (c == 1))


def both_keys(kv_ref, kvo_ref, mask, rows):
    own = jnp.concatenate([kv_ref[rows, :T], mask[1, rows, :]], 1)
    other = jnp.concatenate([kvo_ref[rows, :T], mask[2, rows, :]], 1)
    return jnp.concatenate([own, other], 0)


def turned(w):
    return w.astype(F32).T.astype(BF16)


def attend(ins, outs, scr, export):
    idx_ref, q_ref, kv_ref, kvo_ref, mask = ins[:5]
    o_ref, o_keep, lse, q_keep, kv_keep, kvo_keep, n_keep = outs
    (vt,) = scr
    export(q_ref, q_keep)
    export(kv_ref, kv_keep)
    export(kvo_ref, kvo_keep)
    for r in range(8):
        export(ins[5 + r], n_keep.at[pl.ds(pl.multiple_of(block_place(idx_ref, r) * T, T), T)])
    for i, kv in enumerate((kv_ref, kvo_ref)):
        for b in range(OWN // Q):
            vt[i, :, Q * b : Q * b + Q] = turned(kv[Q * b : Q * b + Q, T:])
    mask = mask.ready()
    masks = diag_masks(idx_ref[0])
    ones = jnp.ones((16, 2 * Q), BF16)

    def query_tile(jt, carry):
        first = pl.multiple_of(jt * Q, Q)
        qrows = pl.ds(first, Q)
        mq = mask[0, qrows, :]
        qa = [jnp.concatenate([h, mq], 1) for h in head_lanes(q_ref[qrows, :])]

        def tile(it, state, diag):
            rows = pl.ds(pl.multiple_of(it * Q, Q), Q)
            v = jnp.concatenate([vt[0, :, rows], vt[1, :, rows]], 1)
            k = [
                jnp.concatenate([kv[rows, :T], mask[1 + i, rows, :]], 1)
                for i, kv in enumerate((kv_ref, kvo_ref))
            ]
            out = []
            for h in range(2):
                m, acc = state[h]
                s = [mm(k[i], qa[h], NT) for i in range(2)]
                if diag:
                    s = [jnp.where(masks[i], s[i], NEG) for i in range(2)]
                top = jnp.max(jnp.maximum(s[0], s[1]), axis=0, keepdims=True)
                m_new = jnp.maximum(m, top)
                p = jnp.concatenate([jnp.exp(v_ - m_new).astype(BF16) for v_ in s], 0)
                vh = jnp.concatenate([v[64 * h : 64 * h + 64], ones], 0)
                out.append((m_new, acc * jnp.exp(m - m_new) + mm(vh, p)))
            return tuple(out)

        zero = (jnp.full((1, Q), NEG, F32), jnp.zeros((80, Q), F32))
        state = tile(jt, (zero, zero), True)
        state = lax.fori_loop(0, jt, lambda it, st: tile(it, st, False), state)
        o = jnp.concatenate([acc[:64] / acc[64:65] for _, acc in state], 0)
        o_keep.ref[:, qrows] = o
        o = o.T.astype(BF16)
        for b in range(Q // T):
            o_ref[jt * (Q // T) + b] = o[b * T : b * T + T]
        for h, (m, acc) in enumerate(state):
            lse.ref[pl.ds(h, 1), qrows] = m + jnp.log(acc[64:65])
        return carry

    lax.fori_loop(0, OWN // Q, query_tile, 0)


DOUBLED = [0, 4, 1, 5, 2, 6, 3, 7]


def middle(ins, outs, scr, export):
    idx_ref, o_ref, own_ref, other_ref, x_l, gains_l = ins
    n2_ref, stat_ref, a_out, h_out, o_out, w_out = outs
    c = idx_ref[0]
    o = jnp.concatenate([o_ref[j] for j in range(8)], 1)
    o_out.ref[...] = o
    o_out.flush()
    for i, r in enumerate(DOUBLED):
        rows = pl.ds(pl.multiple_of(block_place(idx_ref, r) * T, T), T)
        j = DOUBLED.index(r ^ 3 if r % 4 in (1, 2) else r)
        part, part_o = slice(64 * i, 64 * i + 64), slice(64 * j, 64 * j + 64)
        w_out.ref[rows, :] = pair_rows(c, own_ref[part], other_ref[part_o])
    w_out.flush()
    a = mm(o, w_out.ref[...])
    a_out.ref[...] = a
    a_out.flush()
    vhat, _ = norm_parts(a)
    x_ref, gains_ref = x_l.ready(), gains_l.ready()
    h = x_ref[...].astype(F32) + vhat * gains_ref[1:2, :]
    h_out.ref[...] = h
    h_out.flush()
    vhat, _ = norm_parts(h)
    n2_ref[...] = (vhat * gains_ref[2:3, :]).astype(BF16)
    stat_ref[...] = jnp.zeros((8, T), F32) + jnp.sum(a * a) * (1.0 / D)


def gelu_tanh(u):
    return jnp.tanh(GELU_A * (u + GELU_B * u * u * u))


def mlp_forward(ins, outs, scr, export):
    ns, ws = ins[:4], ins[4:8]
    u_ref, n_out, parts = outs[0], outs[1], outs[2:]
    for i, ref in enumerate(ns):
        export(ref, n_out.at[pl.ds(T * i, T)])
    n = jnp.concatenate([r[...] for r in ns], 0)
    zs = []
    for s in range(4):
        u = mm(n, ws[s].ready()[:256], NT)
        u_ref[:, 256 * s : 256 * s + 256] = u
        zs.append((0.5 * u * (1.0 + gelu_tanh(u))).astype(BF16))
    m = mm(jnp.concatenate(zs, 1), jnp.concatenate([w.ready()[256:] for w in ws], 0))
    for i in range(4):
        parts[i][...] = m[T * i : T * i + T].astype(BF16)


def total_of(refs):
    total = refs[0][...].astype(F32)
    for ref in refs[1:]:
        total = total + ref[...].astype(F32)
    return total


def turn_back(ins, outs, scr, export):
    h_ref, gains_ref, up_ref = (v.ready() for v in ins[3:])
    out_ref, g_ref, dc_ref, stat_ref = outs
    m = total_of(ins[:3])
    vhat, inv = norm_parts(m)
    gain = gains_ref[3:4, :]
    dy = up_ref[...].astype(F32)
    g_ref[...] = norm_back(vhat, inv, dy, gain).astype(BF16)
    dc_ref[...] = jnp.sum(dy * vhat, axis=0, keepdims=True)
    stat_ref[...] = jnp.zeros((8, T), F32) + jnp.sum(m * m) * (1.0 / D)
    out_ref[...] = (h_ref[...] + vhat * gain).astype(BF16)


def mlp_backward(ins, outs, scr, export):
    gs, ws, u_ref = ins[:4], ins[4:8], ins[8]
    z_ref, du_ref, parts = outs[0], outs[1], outs[2:]
    g = jnp.concatenate([r[...] for r in gs], 0)
    for s in range(4):
        cols = slice(256 * s, 256 * s + 256)
        u = u_ref[:, cols]
        t = gelu_tanh(u)
        z_ref[:, cols] = (0.5 * u * (1.0 + t)).astype(BF16)
        slope = 0.5 * (1.0 + t) + 0.5 * u * (1.0 - t * t) * GELU_A * (1.0 + 3.0 * GELU_B * u * u)
        du_ref[:, cols] = (mm(g, ws[s].ready()[256:], NT) * slope).astype(BF16)
    dn = mm(du_ref[...], jnp.concatenate([w.ready()[:256] for w in ws], 0))
    for i in range(4):
        parts[i][...] = dn[T * i : T * i + T].astype(BF16)


def mlp_grads(ins, outs, scr, export):
    n_l, z, du, gs = ins[0], ins[1], ins[2], ins[3:]
    send_ref, keep = outs
    g = jnp.concatenate([r[...] for r in gs], 0)
    n = n_l.ready()[...]
    for s, ref, slot in ((1, send_ref, 0), (3, send_ref, 1), (0, keep.ref, 0), (2, keep.ref, 1)):
        cols = slice(256 * s, 256 * s + 256)
        ref[slot, :256] = mm(du[:, cols], n, TN).astype(BF16)
        ref[slot, 256:] = mm(z[:, cols], g, TN).astype(BF16)


def back_middle(ins, outs, scr, export):
    h_ref, a_ref, gains_l, up_l, wo_ref = ins[3:]
    gains_ref, up_ref = gains_l.ready(), up_l.ready()
    do_ref, dc_ref, dh_out, ga_out = outs
    dn = total_of(ins[:3])
    vhat, inv = norm_parts(h_ref.ready()[...])
    dc_ref[1:2, :] = jnp.sum(dn * vhat, axis=0, keepdims=True)
    dh = up_ref[...].astype(F32) + norm_back(vhat, inv, dn, gains_ref[2:3, :])
    dh_out.ref[...] = dh
    dh_out.flush()
    vhat, inv = norm_parts(a_ref.ready()[...])
    dc_ref[0:1, :] = jnp.sum(dh * vhat, axis=0, keepdims=True)
    ga = norm_back(vhat, inv, dh, gains_ref[1:2, :]).astype(BF16)
    ga_out.ref[...] = ga
    ga_out.flush()
    do = mm(ga, wo_ref.ready()[...], NT).astype(BF16)
    for j in range(8):
        do_ref[j] = do[:, T * j : T * j + T]


def attend_back(ins, outs, scr, export):
    idx_ref = ins[0]
    do_ref, q_ref, kv_ref, kvo_ref, o_ref, mask, lse, tab = ins[1:]
    dq_out, oth_out, own_out = outs
    acco, kt = scr
    own_ref = own_out.ref
    kv_ref, kvo_ref, mask = kv_ref.ready(), kvo_ref.ready(), mask.ready()
    for i, kv in enumerate((kv_ref, kvo_ref)):
        for b in range(OWN // Q):
            kt[i, :, Q * b : Q * b + Q] = turned(kv[Q * b : Q * b + Q, :T])
    own_ref[...] = jnp.zeros_like(own_ref)
    acco[...] = jnp.zeros_like(acco)
    masks = jnp.concatenate([jnp.where(v, 1, 0) for v in diag_masks(idx_ref[0])], 0) == 1
    do_ref, q_ref, o_ref, lse, tab = (v.ready() for v in (do_ref, q_ref, o_ref, lse, tab))

    def query_tile(jt, carry):
        qrows = pl.ds(pl.multiple_of(jt * Q, Q), Q)
        do = do_ref[qrows, :]
        q_h, do_h = head_lanes(q_ref[qrows, :]), head_lanes(do)
        mq = mask[0, qrows, :]
        qa = [jnp.concatenate([h, mq], 1) for h in q_h]
        inner = do.astype(F32).T * o_ref[:, qrows]
        delta = [jnp.sum(inner[64 * h : 64 * h + 64], axis=0, keepdims=True) for h in range(2)]
        top = [lse[pl.ds(h, 1), qrows] for h in range(2)]
        q_st, do_st = jnp.concatenate(q_h, 0), jnp.concatenate(do_h, 0)

        def tile(it, dq, diag):
            rows = pl.ds(pl.multiple_of(it * Q, Q), Q)
            k = both_keys(kv_ref, kvo_ref, mask, rows)
            v = jnp.concatenate([kv_ref[rows, T:], kvo_ref[rows, T:]], 0)
            t = jnp.concatenate([kt[0, :, rows], kt[1, :, rows]], 1)
            ps, ss, out = [], [], []
            for h in range(2):
                p = jnp.exp(mm(k, qa[h], NT) - top[h])
                if diag:
                    p = jnp.where(masks, p, 0.0)
                s = (p * (mm(v, do_h[h], NT) - delta[h])).astype(BF16)
                ps.append(p.astype(BF16))
                ss.append(s)
                out.append(dq[h] + mm(t[64 * h : 64 * h + 64], s))
            dk = mm(jnp.concatenate(ss, 1), q_st)
            dv = mm(jnp.concatenate(ps, 1), do_st)
            own_ref[rows, :T] += dk[:Q]
            own_ref[rows, T:] += dv[:Q]
            acco[rows, :T] += dk[Q:]
            acco[rows, T:] += dv[Q:]
            return tuple(out)

        zero = jnp.zeros((64, Q), F32)
        dq = tile(jt, (zero, zero), True)
        dq = lax.fori_loop(0, jt, lambda it, st: tile(it, st, False), dq)
        dq = jnp.concatenate(dq, 0).T * 0.125
        dq_out.ref[qrows, :] = (
            dq * tab[0, qrows, :] + swap_halves(dq * tab[1, qrows, :])
        ).astype(BF16)
        return carry

    lax.fori_loop(0, OWN // Q, query_tile, 0)
    own_out.flush()
    dq_out.flush()
    oth_out.ref[...] = acco[...].astype(BF16)


def input_back(ins, outs, scr, export):
    idx_ref = ins[0]
    dq_ref, own_ref, recv_ref, w_l, turn_l = ins[1:]
    dq_ref, own_ref, recv_ref = dq_ref.ready(), own_ref.ready(), recv_ref.ready()
    g_ref = scr[0]
    g_out, parts = outs[0], outs[1:]
    tab = turn_l.ready()
    both = own_ref[...] + recv_ref[...].astype(F32)
    dk = both[:, :T]
    g_ref[:, :T] = dq_ref[...]
    g_ref[:, T : 2 * T] = (dk * tab[0] + swap_halves(dk * tab[1])).astype(BF16)
    g_ref[:, 2 * T :] = both[:, T:].astype(BF16)
    export(g_ref, g_out)
    w = w_l.ready()[...]
    for half in (4, 0):
        rows = [
            pl.ds(pl.multiple_of(block_place(idx_ref, r) * T, T), T)
            for r in DOUBLED[half : half + 4]
        ]
        out = mm(jnp.concatenate([g_ref[r, :] for r in rows], 0), w)
        parts[half // 4][...] = out.astype(BF16)


def attn_grads(ins, outs, scr, export):
    idx_ref, g_l, n_l, w_l, gains_l, dc12_ref, dc3_ref, stat_a, stat_m = ins
    gains_ref = gains_l.ready()
    send_ref, own_ref = outs
    c = idx_ref[0]
    g, n, w_ref = g_l.ready(), n_l.ready(), w_l.ready()
    dc = jnp.zeros((1, D), F32)
    for i in range(3):
        w = mm(g[:, T * i : T * i + T], n[...], TN)
        dc = dc + jnp.sum(w * w_ref[T * i : T * i + T, :].astype(F32), axis=0, keepdims=True)
        own_ref[64 * i : 64 * i + 64] = jnp.where(c == 0, w[:64], w[64:]).astype(BF16)
        send_ref[64 * i : 64 * i + 64] = jnp.where(c == 0, w[64:], w[:64]).astype(BF16)
    row = lax.broadcasted_iota(jnp.int32, (16, D), 0)
    strip = jnp.zeros((16, D), F32)
    extra = [dc / gains_ref[0:1, :], dc12_ref[0:1, :], dc12_ref[1:2, :], dc3_ref[...]]
    extra += [stat_a[0:1, 0:1], stat_m[0:1, 0:1]]
    for i, v in enumerate(extra):
        strip = jnp.where(row == i, v, strip)
    own_ref[192:] = strip.astype(BF16)
    send_ref[192:] = strip.astype(BF16)


def proj_grads(ins, outs, scr, export):
    idx_ref, o_l, ga_l = ins
    c = idx_ref[0]
    oth, own = outs
    w = scr[0]
    w[...] = mm(o_l.ready()[...], ga_l.ready()[...], TN)
    for i, r in enumerate(DOUBLED):
        base = block_place(idx_ref, r) * T
        mine = pl.ds(pl.multiple_of(base + c * 64, 64), 64)
        other = pl.ds(pl.multiple_of(base + (1 - c) * 64, 64), 64)
        j = DOUBLED.index(r ^ 3 if r % 4 in (1, 2) else r)
        own.ref[64 * i : 64 * i + 64] = w[mine, :].astype(BF16)
        oth[64 * j : 64 * j + 64] = w[other, :].astype(BF16)


def fold(ins, outs, scr, export):
    a, b = ins
    a = a.ready() if isinstance(a, Load) else a
    n = outs[0].shape[0]
    outs[0][...] = a[:n] + b[:n]
    outs[1][...] = a[n:] + b[n:]


def last(ins, outs, scr, export):
    x_ref, dh_l, gains_ref = (v.ready() for v in ins[2:])
    vhat, inv = norm_parts(x_ref[...].astype(F32))
    outs[0][...] = dh_l[...] + norm_back(vhat, inv, total_of(ins[:2]), gains_ref[0:1, :])


def halves_sum(ins, outs, scr, export):
    keep, got = ins[0].ready(), ins[1]
    outs[0].ref[...] = keep[0] + got[0]
    other = keep[1] + got[1]
    outs[1][...] = other[:256]
    outs[2][...] = other[256:]


def ring_blocks(idx_ref, whole, outs, n, extra=None):
    at = lambda i: pl.ds(pl.multiple_of(idx_ref[6 + i] * n, n), n)
    m = n if extra is None else n + extra.shape[0]
    for i, (ref, first) in enumerate(((outs[0], 0), (outs[1], 0), (outs[2], 0), (outs[2], m))):
        ref[first : first + n] = whole[at(i), :]
        if extra is not None:
            ref[first + n : first + m] = extra


def mlp_blocks(ins, outs, scr, export):
    idx_ref, mine, inner, outer = ins
    mine = mine.ready()
    scr[0][:256] = mine[:256] + inner[...]
    scr[0][256:] = mine[256:] + outer[...]
    ring_blocks(idx_ref, scr[0], outs, 128)


def attn_blocks(ins, outs, scr, export):
    idx_ref, own, got, *proj = ins
    scr[0][:192] = own[:192] + got[:192]
    scr[0][192:] = total_of(proj).astype(BF16)
    ring_blocks(idx_ref, scr[0], outs, 64, own[192:] + got[192:])


def spread(ins, outs, scr, export):
    idx_ref = ins[0]
    n = scr[0].shape[1]
    for r in range(4):
        scr[0][idx_ref[6 + r]] = ins[1 + r][:n].astype(F32)
    rows = 0
    for ref in outs:
        for i in range(ref.shape[0] // n):
            export(scr[0].at[rows], ref.at[pl.ds(i * n, n)])
            rows += 1


def data_sum(idx, own, a, got, n, shapes):
    m = own.shape[0]
    mine = own + got[:m] + side_a(a + got[m:], "z")
    mine = mine + lax.ppermute(mine, "yh", SWAP)
    return mine, call(
        spread,
        1,
        [("S", idx)] + [("V", v) for v in ring_gather(mine, "z")],
        [("X", s, F32) for s in shapes],
        scratch=[pltpu.VMEM((4, n, D), F32)],
        exports=4,
    )


def after(values, event):
    return lax.optimization_barrier((*values, event))[: len(values)]


def on_device(x, lengths, gains, wq, wk, wv, wo, wup, wdown, upstream):
    c, yl, xi, z = (lax.axis_index(n) for n in ("c", "yl", "x", "z"))

    def ring(i):
        first, second = i ^ 1, (i + 2 * (i & 1) + 3) & 3
        return [i, jnp.where(c == 0, first, second), jnp.where(c == 0, second, first), i ^ 2]

    idx = jnp.stack([c, yl, *ring(xi), *ring(z)]).astype(jnp.int32)
    freq = (10000.0 ** (-2.0 * np.arange(32) / 64.0)).astype(np.float32)
    freq = jnp.asarray(np.tile(freq, 4)[None, :])
    bf = lambda k, *s: (k, s, BF16)
    f32 = lambda k, *s: (k, s, F32)
    many = lambda k, arrays: [(k, a) for a in arrays]
    I = ("S", idx)
    G, X, U = ("H", gains), ("H", x), ("H", upstream)

    (n1,) = call(first_norm, 1.0, [X, G], [bf("H", T, D)], vmem=60)
    n1 = chip_gather(n1)
    wqkv, w_own = call(
        pack, 1.0, many("R", (wq, wk, wv, wup, wdown)), [bf("V", 192, D), bf("X", 512, D)], exports=5
    )
    wqkv_o = core(wqkv)
    w_core = core(w_own)
    w_y = lax.ppermute(w_own, ("yh", "yl"), OUTER)
    wo_all = stack(wo, side_y(wo))
    wo_all = stack(wo_all, side_a(wo_all, "x"))
    wo_b = side_b(wo_all, "x")
    turn, mask, turn_keep = call(
        tables,
        3,
        [I, ("S", lengths), ("V", freq)],
        [f32("V", 2, OWN, T), bf("H", 3, OWN, T), f32("X", 2, OWN, T)],
        exports=1,
    )
    q, kv, w_pair = call(
        qkv,
        3.0,
        [I, ("V", wqkv), ("V", wqkv_o), ("V", turn)] + many("V", n1),
        [bf("V", OWN, T), bf("V", OWN, 2 * T), bf("H", 3 * T, D)],
    )
    kvo = core(kv)
    q, w_core, w_y = after([q, w_core, w_y], kvo)
    o, o32, lse, q_keep, kv_keep, kvo_keep, n1_all = call(
        attend,
        100.0,
        [I, ("V", q), ("V", kv), ("V", kvo), ("H", mask)] + many("V", n1),
        [
            bf("V", 8, T, T),
            f32("H", T, OWN),
            f32("H", 8, OWN),
            bf("X", OWN, T),
            bf("X", OWN, 2 * T),
            bf("X", OWN, 2 * T),
            bf("X", OWN, D),
        ],
        scratch=[pltpu.VMEM((2, T, OWN), BF16)],
        exports=11,
    )
    (wo_b,) = after([wo_b], o)
    wo_all = stack(wo_all, wo_b)
    (o,) = after([o], wo_all)
    wo_c = core(wo_all)
    o_all = lax.all_to_all(o, ("yl", "x"), 0, 0, tiled=True)
    n2, stat_a, a, h, o_full, wo_full = call(
        middle,
        2.0,
        [I, ("V", o_all), ("V", wo_all), ("V", wo_c), X, G],
        [bf("V", T, D), f32("V", 8, T), f32("H", T, D), f32("H", T, D), bf("H", T, D), bf("H", D, D)],
    )
    (w_y,) = after([w_y], n2)
    ws = many("H", (w_own, w_core, w_y, core(w_y)))
    u, n2_all, *parts = call(
        mlp_forward,
        4.0,
        many("V", ring_gather(n2, "x")) + ws,
        [f32("V", 4 * T, D), bf("X", 4 * T, D)] + [bf("V", T, D)] * 4,
        vmem=24,
        exports=4,
    )
    terms, _ = ring_scatter(parts, "x")
    block_out, gm, dc3, stat_m = call(
        turn_back,
        1.0,
        many("V", terms) + [("H", h), G, U],
        [bf("V", T, D), bf("V", T, D), f32("V", 1, D), f32("V", 8, T)],
    )
    gm = ring_gather(gm, "x")
    zz, du, *parts = call(
        mlp_backward,
        4.0,
        many("V", gm) + ws + [("V", u)],
        [bf("V", 4 * T, D), bf("V", 4 * T, D)] + [bf("V", T, D)] * 4,
        vmem=24,
    )
    terms, passed = ring_scatter(parts, "x")
    zz, du = after([zz, du], passed)
    send, keep = call(
        mlp_grads,
        30.0,
        [("H", n2_all), ("V", zz), ("V", du)] + many("V", gm),
        [bf("V", 2, 512, D), bf("H", 2, 512, D)],
    )
    got = core(send)
    do, dc12, dh, ga = call(
        back_middle,
        30.0,
        many("V", terms) + [("H", h), ("H", a), G, U, ("H", wo_full)],
        [bf("V", 8, T, T), f32("V", 2, D), f32("H", T, D), bf("H", T, D)],
    )
    mine, oa, ob = call(
        halves_sum, 1.0, [("H", keep), ("V", got)], [bf("H", 512, D), bf("V", 256, D), bf("V", 256, D)]
    )
    inner = side_y(oa)
    outer = lax.ppermute(ob, ("yh", "yl"), OUTER)
    (do,) = after([do], oa)
    do_all = lax.all_to_all(do, ("yl", "x"), 0, 0, tiled=True).reshape(OWN, T)
    po_send, po = call(
        proj_grads,
        2.0,
        [I, ("H", o_full), ("H", ga)],
        [bf("V", 512, D), bf("H", 512, D)],
        scratch=[pltpu.VMEM((D, D), F32)],
    )
    po_got = core(po_send)
    po, po_send = call(fold, 1.0, [("H", po), ("V", po_got)], [bf("V", 256, D)] * 2)
    (do_all,) = after([do_all], (oa, po_send))
    po_got = side_b(po_send, "x")
    dq, oth, own32 = call(
        attend_back,
        10,
        [I] + many("H", (do_all, q_keep, kv_keep, kvo_keep, o32, mask, lse, turn_keep)),
        [bf("H", OWN, T), bf("H", OWN, 2 * T), f32("H", OWN, 2 * T)],
        scratch=[pltpu.VMEM((OWN, 2 * T), F32), pltpu.VMEM((2, T, OWN), BF16)],
        vmem=60,
    )
    (oth,) = after([oth], (inner, outer, po_got))
    recv = core(oth)
    inner, outer, po_got = after([inner, outer, po_got], oth)
    m_blocks = call(
        mlp_blocks,
        1.0,
        [I, ("H", mine), ("V", inner), ("V", outer)],
        [bf("V", 128, D), bf("V", 128, D), bf("V", 256, D)],
        scratch=[pltpu.VMEM((512, D), BF16)],
    )
    got_z = side_b(m_blocks[2], "z")
    dqkv, part, part_send = call(
        input_back,
        2.0,
        [I] + many("H", (dq, own32, recv, w_pair, turn_keep)),
        [bf("X", OWN, 3 * T), bf("V", 4 * T, D), bf("V", 4 * T, D)],
        scratch=[pltpu.VMEM((OWN, 3 * T), BF16)],
        exports=1,
    )
    part, part_send = call(
        fold, 1.0, many("V", (part, side_b(part_send, "x"))), [bf("V", 2 * T, D)] * 2
    )
    part, part_send = call(
        fold, 1.0, many("V", (part, side_a(part_send, "x"))), [bf("V", T, D)] * 2
    )
    g_send, g_own = call(
        attn_grads,
        2.0,
        [I, ("H", dqkv), ("H", n1_all), ("H", w_pair), G] + many("V", (dc12, dc3, stat_a, stat_m)),
        [bf("V", 208, D), bf("V", 208, D)],
    )
    g_recv = core(g_send)
    (input_grad,) = call(
        last, 1.0, many("V", (part, side_y(part_send))) + [X, ("H", dh), G], [f32("V", T, D)]
    )
    _, (g_up, g_down) = data_sum(idx, m_blocks[0], m_blocks[1], got_z, 128, [(256, D), (256, D)])

    po, po_send = call(fold, 1.0, many("V", (po, po_got)), [bf("V", 128, D)] * 2)
    po, po_send = call(fold, 1.0, many("V", (po, side_a(po_send, "x"))), [bf("V", 64, D)] * 2)
    blocks = call(
        attn_blocks,
        1.0,
        [I] + many("V", (g_own, g_recv, po, side_y(po_send))),
        [bf("V", 80, D), bf("V", 80, D), bf("V", 160, D)],
        scratch=[pltpu.VMEM((256, D), BF16)],
    )
    mine, (g_q, g_k, g_v, g_o) = data_sum(
        idx, blocks[0], blocks[1], side_b(blocks[2], "z"), 64, [(64, D)] * 4
    )

    rows = mine[64:72].astype(F32)
    rows = rows + side_a(rows, "x")
    rows = rows + side_b(rows, "x")
    rows = rows + side_y(rows)
    stats = rows[4:6, 0] * (1.0 / 16384.0)
    return block_out, input_grad, g_q, g_k, g_v, g_o, g_up, g_down, rows[:4], stats


def solution(mesh):
    names = ("yh", "z", "yl", "x", "c")
    fine = Mesh(np.asarray(mesh.devices).reshape(2, 4, 2, 4, 2), names)
    tokens, group, shard = P(names, None), P(("yh", "z"), None), P(("yl", "x", "c"), None)
    return jax.shard_map(
        on_device,
        mesh=fine,
        in_specs=(tokens, group, P(), shard, shard, shard, shard, shard, shard, tokens),
        out_specs=(tokens, tokens, shard, shard, shard, shard, shard, shard, P(), P()),
        check_vma=False,
    )
```

```python
import functools

import jax
import jax.numpy as jnp
import numpy as np
from jax import lax
from jax.experimental import pallas as pl
from jax.experimental.pallas import tpu as pltpu
from jax.sharding import Mesh
from jax.sharding import PartitionSpec as P

D = 1024
T = 128
NB = 8
OWN = NB * T
F32 = jnp.float32
BF16 = jnp.bfloat16
NEG = -1e30
EPS = 1e-05
MATCH = ([(0, 1), (1, 0), (2, 3), (3, 2)], [(1, 2), (2, 1), (3, 0), (0, 3)])
SIDE_A = [(2 * i + c, 2 * j + c) for c in range(2) for i, j in MATCH[c]]
SIDE_B = [(2 * i + c, 2 * j + c) for c in range(2) for i, j in MATCH[1 - c]]
SWAP = [(0, 1), (1, 0)]
OUTER = [(0, 3), (3, 0), (1, 2), (2, 1)]
NT = (((1,), (1,)), ((), ()))
NN = (((1,), (0,)), ((), ()))
TN = (((0,), (0,)), ((), ()))
GELU_A = float(np.sqrt(2.0 / np.pi))
GELU_B = 0.044715


def mm(a, b, dims=NN):
    return lax.dot_general(a, b, dims, preferred_element_type=F32)


class Load:
    def __init__(self, src, dst, sem):
        self.copy, self.dst, self.waited = pltpu.make_async_copy(src, dst, sem), dst, False
        self.copy.start()

    def ready(self):
        if not self.waited:
            self.copy.wait()
            self.waited = True
        return self.dst


class Store:
    def __init__(self, src, dst, sem):
        self.copy, self.ref, self.sent = pltpu.make_async_copy(src, dst, sem), src, False

    def flush(self):
        if not self.sent:
            self.copy.start()
            self.sent = True


def call(body, us, ins, outs, vmem=16, scratch=(), exports=0):
    space = {"S": pltpu.SMEM, "V": pltpu.VMEM, "H": pltpu.HBM, "X": pltpu.HBM, "R": pltpu.HBM}
    kinds_in, kinds_out = [k for k, _ in ins], [k for k, _, _ in outs]
    buffers = [pltpu.VMEM(a.shape, a.dtype) for k, a in ins if k == "H"]
    buffers += [pltpu.VMEM(s, d) for k, s, d in outs if k == "H"]
    n_sems = len(buffers) + exports

    def kernel(*refs):
        refs = list(refs)
        n_in, n_out = len(ins), len(outs)
        raw_in, raw_out = refs[:n_in], refs[n_in : n_in + n_out]
        held = refs[n_in + n_out : n_in + n_out + len(buffers)]
        rest = refs[n_in + n_out + len(buffers) :]
        if n_sems:
            sems, rest = rest[0], rest[1:]
        used = [0]
        exported = []

        def sem():
            used[0] += 1
            return sems.at[used[0] - 1]

        def export(src, dst):
            copy = pltpu.make_async_copy(src, dst, sem())
            copy.start()
            exported.append(copy)

        held = list(held)
        loads = [Load(r, held.pop(0), sem()) if k == "H" else r for k, r in zip(kinds_in, raw_in)]
        stores = [Store(held.pop(0), r, sem()) if k == "H" else r for k, r in zip(kinds_out, raw_out)]
        body(loads, stores, rest, export)
        for s in stores:
            if isinstance(s, Store):
                s.flush()
        for v in loads:
            if isinstance(v, Load):
                v.ready()
        for s in stores:
            if isinstance(s, Store):
                s.copy.wait()
        for copy in exported:
            copy.wait()

    return pl.pallas_call(
        kernel,
        out_shape=tuple(jax.ShapeDtypeStruct(s, d) for _, s, d in outs),
        in_specs=[pl.BlockSpec(memory_space=space[k]) for k in kinds_in],
        out_specs=tuple(pl.BlockSpec(memory_space=space[k]) for k in kinds_out),
        scratch_shapes=buffers + ([pltpu.SemaphoreType.DMA((n_sems,))] if n_sems else []) + list(scratch),
        compiler_params=pltpu.CompilerParams(vmem_limit_bytes=vmem << 20),
        cost_estimate=pl.CostEstimate(flops=int(us * 1.1e9), bytes_accessed=0, transcendentals=0),
    )(*[a for _, a in ins])


def side_a(v, axis):
    return lax.ppermute(v, (axis, "c"), SIDE_A)


def side_b(v, axis):
    return lax.ppermute(v, (axis, "c"), SIDE_B)


def side_y(v):
    return lax.ppermute(v, "yl", SWAP)


def core(v):
    return lax.ppermute(v, "c", SWAP)


def ring_gather(own, axis):
    a = side_a(own, axis)
    b = side_b(own, axis)
    return [own, a, b, side_b(a, axis)]


def ring_scatter(parts, axis):
    own, a, b, f = parts
    got = side_b(f, axis)
    other = side_b(b, axis)
    passed = a + got
    return [own, other, side_a(passed, axis)], passed


def chip_gather(own):
    y = side_y(own)
    row = ring_gather(own, "x")
    return row + [y, side_a(y, "x"), side_b(y, "x"), side_y(row[3])]


def norm_parts(v):
    center = v - jnp.mean(v, axis=-1, keepdims=True)
    inv = lax.rsqrt(jnp.mean(center * center, axis=-1, keepdims=True) + EPS)
    return center * inv, inv


def norm_back(vhat, inv, grad, gain):
    t = grad * gain
    return inv * (
        t
        - jnp.mean(t, axis=-1, keepdims=True)
        - vhat * jnp.mean(t * vhat, axis=-1, keepdims=True)
    )


def first_norm(ins, outs, scr, export):
    x, gains = (v.ready() for v in ins)
    vhat, _ = norm_parts(x[...].astype(F32))
    outs[0].ref[...] = (vhat * gains[0:1, :]).astype(BF16)


def stack(*arrays):
    rows = [v.shape[0] for v in arrays]

    def body(ins, outs, scr, export):
        at = 0
        for ref, n in zip(ins, rows):
            outs[0][at : at + n] = ref[...]
            at += n

    return call(body, 1, [("V", v) for v in arrays], [("V", (sum(rows), D), BF16)])[0]


def pack(ins, outs, scr, export):
    at = [0, 0]
    for i, ref in enumerate(ins):
        o = 0 if i < 3 else 1
        export(ref, outs[o].at[pl.ds(at[o], ref.shape[0])])
        at[o] += ref.shape[0]


def own_places(parity, rows):
    i = lax.broadcasted_iota(jnp.int32, (rows, T), 0)
    return ((i // T) * 2 + parity) * T + i % T


def row_of(ends_ref, places):
    row = jnp.zeros_like(places)
    start = jnp.zeros_like(places)
    end = jnp.int32(0)
    for k in range(8):
        end = end + ends_ref[0, k]
        inside = places >= end
        row = row + jnp.where(inside, 1, 0)
        start = jnp.where(inside, end, start)
    return row, places - start


def tables(ins, outs, scr, export):
    idx_ref, len_ref, freq_ref = ins
    turn, mask_out, turn_keep = outs
    c = idx_ref[0]
    n = OWN // 4
    lane = lax.broadcasted_iota(jnp.int32, (n, T), 1)
    token = lax.broadcasted_iota(jnp.int32, (n, T), 0) + (lane // 32) * n
    _, pos = row_of(len_ref, ((token // T) * 2 + c) * T + token % T)
    angle = pos.astype(F32) * freq_ref[...]
    for i, v in enumerate((jnp.cos(angle), jnp.sin(angle))):
        for g in range(4):
            w = jnp.where(lane // 32 == g, v, 0.0)
            w = w + pltpu.roll(w, 32, 1)
            w = w + pltpu.roll(w, 64, 1)
            if i == 1:
                w = jnp.where(lane % 64 < 32, -w, w)
            turn[i, n * g : n * g + n] = w
    export(turn, turn_keep)
    lane = lax.broadcasted_iota(jnp.int32, (OWN, T), 1)
    row, _ = row_of(len_ref, own_places(c, OWN))
    mask_out.ref[0] = jnp.where((lane < 8) & (lane != row), NEG, 0.0).astype(BF16)
    mask_out.ref[1] = jnp.where(lane == row, 1.0, 0.0).astype(BF16)
    row, _ = row_of(len_ref, own_places(1 - c, OWN))
    mask_out.ref[2] = jnp.where(lane == row, 1.0, 0.0).astype(BF16)


def swap_halves(w):
    lane = lax.broadcasted_iota(jnp.int32, w.shape, 1)
    return jnp.where(lane % 64 < 32, pltpu.roll(w, 96, 1), pltpu.roll(w, 32, 1))


def pair_rows(c, own, other):
    first = jnp.where(c == 0, own, other)
    second = jnp.where(c == 0, other, own)
    return jnp.concatenate([first, second], 0)


def block_place(idx_ref, r):
    yl = idx_ref[1] if r < 4 else 1 - idx_ref[1]
    return yl * 4 + idx_ref[2 + r % 4]


def qkv(ins, outs, scr, export):
    idx_ref, own_ref, other_ref, turn = ins[:4]
    blocks = ins[4:]
    q_ref, kv_ref, w_out = outs
    c = idx_ref[0]
    w = jnp.concatenate(
        [
            pair_rows(c, own_ref[64 * i : 64 * i + 64], other_ref[64 * i : 64 * i + 64])
            for i in range(3)
        ],
        0,
    )
    w_out.ref[...] = w
    w_out.flush()
    for half in (0, 4):
        out = mm(jnp.concatenate([v[...] for v in blocks[half : half + 4]], 0), w, NT)
        for i in range(4):
            rows = pl.ds(pl.multiple_of(block_place(idx_ref, half + i) * T, T), T)
            part = out[T * i : T * i + T]
            cos, sin = turn[0, rows, :], turn[1, rows, :]
            q, k = part[:, :T], part[:, T : 2 * T]
            q_ref[rows, :] = ((q * cos + swap_halves(q) * sin) * 0.125).astype(BF16)
            kv_ref[rows, :T] = (k * cos + swap_halves(k) * sin).astype(BF16)
            kv_ref[rows, T:] = part[:, 2 * T :].astype(BF16)


Q = 256


def head_lanes(w):
    lane = lax.broadcasted_iota(jnp.int32, w.shape, 1)
    fill = jnp.zeros_like(w)
    return jnp.where(lane < 64, w, fill), jnp.where(lane < 64, fill, w)


def diag_masks(c):
    k = lax.broadcasted_iota(jnp.int32, (Q, Q), 0)
    i = lax.broadcasted_iota(jnp.int32, (Q, Q), 1)
    kb, ib = k // T, i // T
    return k <= i, (kb < ib) | ((kb == ib) & (c == 1))


def visible(s, masks, other):
    n = s.shape[0] // 2
    own = jnp.where(masks[0], s[n - Q : n], other)
    parts = [own, jnp.where(masks[1], s[2 * n - Q :], other)]
    if n > Q:
        parts = [s[: n - Q], parts[0], s[n : 2 * n - Q], parts[1]]
    return jnp.concatenate(parts, 0)


def both_keys(kv_ref, kvo_ref, mask, rows):
    own = jnp.concatenate([kv_ref[rows, :T], mask[1, rows, :]], 1)
    other = jnp.concatenate([kvo_ref[rows, :T], mask[2, rows, :]], 1)
    return jnp.concatenate([own, other], 0)


def turned(w):
    return w.astype(F32).T.astype(BF16)


def attend(ins, outs, scr, export):
    idx_ref, q_ref, kv_ref, kvo_ref, mask = ins[:5]
    o_ref, o_keep, lse, q_keep, kv_keep, kvo_keep, n_keep = outs
    (vt,) = scr
    export(q_ref, q_keep)
    export(kv_ref, kv_keep)
    export(kvo_ref, kvo_keep)
    for r in range(8):
        export(ins[5 + r], n_keep.at[pl.ds(pl.multiple_of(block_place(idx_ref, r) * T, T), T)])
    for i, kv in enumerate((kv_ref, kvo_ref)):
        for b in range(OWN // Q):
            vt[i, :, Q * b : Q * b + Q] = turned(kv[Q * b : Q * b + Q, T:])
    mask = mask.ready()
    masks = diag_masks(idx_ref[0])
    ones = jnp.ones((16, 2 * Q), BF16)

    for jt in range(OWN // Q):
        qrows = slice(jt * Q, jt * Q + Q)
        mq = mask[0, qrows, :]
        qa = [jnp.concatenate([h, mq], 1) for h in head_lanes(q_ref[qrows, :])]

        def tile(it, state, diag):
            rows = slice(it * Q, it * Q + Q)
            v = jnp.concatenate([vt[0, :, rows], vt[1, :, rows]], 1)
            k = [
                jnp.concatenate([kv[rows, :T], mask[1 + i, rows, :]], 1)
                for i, kv in enumerate((kv_ref, kvo_ref))
            ]
            out = []
            for h in range(2):
                m, acc = state[h]
                s = [mm(k[i], qa[h], NT) for i in range(2)]
                if diag:
                    s = [jnp.where(masks[i], s[i], NEG) for i in range(2)]
                top = jnp.max(jnp.maximum(s[0], s[1]), axis=0, keepdims=True)
                m_new = jnp.maximum(m, top)
                p = jnp.concatenate([jnp.exp(v_ - m_new).astype(BF16) for v_ in s], 0)
                vh = jnp.concatenate([v[64 * h : 64 * h + 64], ones], 0)
                out.append((m_new, acc * jnp.exp(m - m_new) + mm(vh, p)))
            return tuple(out)

        zero = (jnp.full((1, Q), NEG, F32), jnp.zeros((80, Q), F32))
        state = tile(jt, (zero, zero), True)
        for it in range(jt):
            state = tile(it, state, False)
        o = jnp.concatenate([acc[:64] / acc[64:65] for _, acc in state], 0)
        o_keep.ref[:, qrows] = o
        o = o.T.astype(BF16)
        for b in range(Q // T):
            o_ref[jt * (Q // T) + b] = o[b * T : b * T + T]
        for h, (m, acc) in enumerate(state):
            lse.ref[h : h + 1, qrows] = m + jnp.log(acc[64:65])


DOUBLED = [0, 4, 1, 5, 2, 6, 3, 7]


def middle(ins, outs, scr, export):
    idx_ref, o_ref, own_ref, other_ref, x_l, gains_l = ins
    n2_ref, stat_ref, a_out, h_out, o_out, w_out = outs
    c = idx_ref[0]
    o = jnp.concatenate([o_ref[j] for j in range(8)], 1)
    o_out.ref[...] = o
    o_out.flush()
    for i, r in enumerate(DOUBLED):
        rows = pl.ds(pl.multiple_of(block_place(idx_ref, r) * T, T), T)
        j = DOUBLED.index(r ^ 3 if r % 4 in (1, 2) else r)
        part, part_o = slice(64 * i, 64 * i + 64), slice(64 * j, 64 * j + 64)
        w_out.ref[rows, :] = pair_rows(c, own_ref[part], other_ref[part_o])
    w_out.flush()
    a = mm(o, w_out.ref[...])
    a_out.ref[...] = a
    a_out.flush()
    vhat, _ = norm_parts(a)
    x_ref, gains_ref = x_l.ready(), gains_l.ready()
    h = x_ref[...].astype(F32) + vhat * gains_ref[1:2, :]
    h_out.ref[...] = h
    h_out.flush()
    vhat, _ = norm_parts(h)
    n2_ref[...] = (vhat * gains_ref[2:3, :]).astype(BF16)
    stat_ref[...] = jnp.zeros((8, T), F32) + jnp.sum(a * a) * (1.0 / D)


def gelu_tanh(u):
    return jnp.tanh(GELU_A * (u + GELU_B * u * u * u))


def mlp_forward(ins, outs, scr, export):
    ns, ws = ins[:4], ins[4:8]
    u_ref, n_out, parts = outs[0], outs[1], outs[2:]
    for i, ref in enumerate(ns):
        export(ref, n_out.at[pl.ds(T * i, T)])
    n = jnp.concatenate([r[...] for r in ns], 0)
    zs = []
    for s in range(4):
        u = mm(n, ws[s].ready()[:256], NT)
        u_ref[:, 256 * s : 256 * s + 256] = u
        zs.append((0.5 * u * (1.0 + gelu_tanh(u))).astype(BF16))
    m = mm(jnp.concatenate(zs, 1), jnp.concatenate([w.ready()[256:] for w in ws], 0))
    for i in range(4):
        parts[i][...] = m[T * i : T * i + T].astype(BF16)


def total_of(refs):
    total = refs[0][...].astype(F32)
    for ref in refs[1:]:
        total = total + ref[...].astype(F32)
    return total


def turn_back(ins, outs, scr, export):
    h_ref, gains_ref, up_ref = (v.ready() for v in ins[3:])
    out_ref, g_ref, dc_ref, stat_ref = outs
    m = total_of(ins[:3])
    vhat, inv = norm_parts(m)
    gain = gains_ref[3:4, :]
    dy = up_ref[...].astype(F32)
    g_ref[...] = norm_back(vhat, inv, dy, gain).astype(BF16)
    dc_ref[...] = jnp.sum(dy * vhat, axis=0, keepdims=True)
    stat_ref[...] = jnp.zeros((8, T), F32) + jnp.sum(m * m) * (1.0 / D)
    out_ref[...] = (h_ref[...] + vhat * gain).astype(BF16)


def mlp_backward(ins, outs, scr, export):
    gs, ws, u_ref = ins[:4], ins[4:8], ins[8]
    z_ref, du_ref, parts = outs[0], outs[1], outs[2:]
    g = jnp.concatenate([r[...] for r in gs], 0)
    for s in range(4):
        cols = slice(256 * s, 256 * s + 256)
        u = u_ref[:, cols]
        t = gelu_tanh(u)
        z_ref[:, cols] = (0.5 * u * (1.0 + t)).astype(BF16)
        slope = 0.5 * (1.0 + t) + 0.5 * u * (1.0 - t * t) * GELU_A * (1.0 + 3.0 * GELU_B * u * u)
        du_ref[:, cols] = (mm(g, ws[s].ready()[256:], NT) * slope).astype(BF16)
    dn = mm(du_ref[...], jnp.concatenate([w.ready()[:256] for w in ws], 0))
    for i in range(4):
        parts[i][...] = dn[T * i : T * i + T].astype(BF16)


def mlp_grads(ins, outs, scr, export):
    n_l, z, du, gs = ins[0], ins[1], ins[2], ins[3:]
    send_ref, keep = outs
    g = jnp.concatenate([r[...] for r in gs], 0)
    n = n_l.ready()[...]
    for s, ref, slot in ((1, send_ref, 0), (3, send_ref, 1), (0, keep.ref, 0), (2, keep.ref, 1)):
        cols = slice(256 * s, 256 * s + 256)
        ref[slot, :256] = mm(du[:, cols], n, TN).astype(BF16)
        ref[slot, 256:] = mm(z[:, cols], g, TN).astype(BF16)


def back_middle(ins, outs, scr, export):
    h_ref, a_ref, gains_l, up_l, wo_ref = ins[3:]
    gains_ref, up_ref = gains_l.ready(), up_l.ready()
    do_ref, dc_ref, dh_out, ga_out = outs
    dn = total_of(ins[:3])
    vhat, inv = norm_parts(h_ref.ready()[...])
    dc_ref[1:2, :] = jnp.sum(dn * vhat, axis=0, keepdims=True)
    dh = up_ref[...].astype(F32) + norm_back(vhat, inv, dn, gains_ref[2:3, :])
    dh_out.ref[...] = dh
    dh_out.flush()
    vhat, inv = norm_parts(a_ref.ready()[...])
    dc_ref[0:1, :] = jnp.sum(dh * vhat, axis=0, keepdims=True)
    ga = norm_back(vhat, inv, dh, gains_ref[1:2, :]).astype(BF16)
    ga_out.ref[...] = ga
    ga_out.flush()
    do = mm(ga, wo_ref.ready()[...], NT).astype(BF16)
    for j in range(8):
        do_ref[j] = do[:, T * j : T * j + T]


def attend_back(ins, outs, scr, export):
    idx_ref = ins[0]
    do_ref, q_ref, kv_ref, kvo_ref, o_ref, mask, lse, tab = ins[1:]
    dq_out, oth_out, own_out = outs
    acco, kt = scr
    own_ref = own_out.ref
    kv_ref, kvo_ref, mask = kv_ref.ready(), kvo_ref.ready(), mask.ready()
    for i, kv in enumerate((kv_ref, kvo_ref)):
        for b in range(OWN // Q):
            kt[i, :, Q * b : Q * b + Q] = turned(kv[Q * b : Q * b + Q, :T])
    own_ref[...] = jnp.zeros_like(own_ref)
    acco[...] = jnp.zeros_like(acco)
    masks = diag_masks(idx_ref[0])
    do_ref, q_ref, o_ref, lse, tab = (v.ready() for v in (do_ref, q_ref, o_ref, lse, tab))

    for jt in range(OWN // Q):
        qrows = slice(jt * Q, jt * Q + Q)
        do = do_ref[qrows, :]
        q_h, do_h = head_lanes(q_ref[qrows, :]), head_lanes(do)
        mq = mask[0, qrows, :]
        qa = [jnp.concatenate([h, mq], 1) for h in q_h]
        inner = do.astype(F32).T * o_ref[:, qrows]
        delta = [jnp.sum(inner[64 * h : 64 * h + 64], axis=0, keepdims=True) for h in range(2)]
        top = [lse[h : h + 1, qrows] for h in range(2)]
        q_st, do_st = jnp.concatenate(q_h, 0), jnp.concatenate(do_h, 0)

        n = jt * Q + Q
        k = both_keys(kv_ref, kvo_ref, mask, slice(0, n))
        v = jnp.concatenate([kv_ref[:n, T:], kvo_ref[:n, T:]], 0)
        t = jnp.concatenate([kt[0, :, :n], kt[1, :, :n]], 1)
        ps, ss, dq = [], [], []
        for h in range(2):
            p = visible(jnp.exp(mm(k, qa[h], NT) - top[h]), masks, 0.0)
            s = (p * (mm(v, do_h[h], NT) - delta[h])).astype(BF16)
            ps.append(p.astype(BF16))
            ss.append(s)
            dq.append(mm(t[64 * h : 64 * h + 64], s))
        dk = mm(jnp.concatenate(ss, 1), q_st)
        dv = mm(jnp.concatenate(ps, 1), do_st)
        own_ref[:n, :T] += dk[:n]
        own_ref[:n, T:] += dv[:n]
        acco[:n, :T] += dk[n:]
        acco[:n, T:] += dv[n:]
        dq = jnp.concatenate(dq, 0).T * 0.125
        dq_out.ref[qrows, :] = (
            dq * tab[0, qrows, :] + swap_halves(dq * tab[1, qrows, :])
        ).astype(BF16)

    own_out.flush()
    dq_out.flush()
    oth_out.ref[...] = acco[...].astype(BF16)


def input_back(ins, outs, scr, export):
    idx_ref = ins[0]
    dq_ref, own_ref, recv_ref, w_l, turn_l = ins[1:]
    dq_ref, own_ref, recv_ref = dq_ref.ready(), own_ref.ready(), recv_ref.ready()
    g_ref = scr[0]
    g_out, parts = outs[0], outs[1:]
    tab = turn_l.ready()
    both = own_ref[...] + recv_ref[...].astype(F32)
    dk = both[:, :T]
    g_ref[:, :T] = dq_ref[...]
    g_ref[:, T : 2 * T] = (dk * tab[0] + swap_halves(dk * tab[1])).astype(BF16)
    g_ref[:, 2 * T :] = both[:, T:].astype(BF16)
    export(g_ref, g_out)
    w = w_l.ready()[...]
    for half in (4, 0):
        rows = [
            pl.ds(pl.multiple_of(block_place(idx_ref, r) * T, T), T)
            for r in DOUBLED[half : half + 4]
        ]
        out = mm(jnp.concatenate([g_ref[r, :] for r in rows], 0), w)
        parts[half // 4][...] = out.astype(BF16)


def attn_grads(ins, outs, scr, export):
    idx_ref, g_l, n_l, w_l, gains_l, dc12_ref, dc3_ref, stat_a, stat_m = ins
    gains_ref = gains_l.ready()
    send_ref, own_ref = outs
    c = idx_ref[0]
    g, n, w_ref = g_l.ready(), n_l.ready(), w_l.ready()
    dc = jnp.zeros((1, D), F32)
    for i in range(3):
        w = mm(g[:, T * i : T * i + T], n[...], TN)
        dc = dc + jnp.sum(w * w_ref[T * i : T * i + T, :].astype(F32), axis=0, keepdims=True)
        own_ref[64 * i : 64 * i + 64] = jnp.where(c == 0, w[:64], w[64:]).astype(BF16)
        send_ref[64 * i : 64 * i + 64] = jnp.where(c == 0, w[64:], w[:64]).astype(BF16)
    row = lax.broadcasted_iota(jnp.int32, (16, D), 0)
    strip = jnp.zeros((16, D), F32)
    extra = [dc / gains_ref[0:1, :], dc12_ref[0:1, :], dc12_ref[1:2, :], dc3_ref[...]]
    extra += [stat_a[0:1, 0:1], stat_m[0:1, 0:1]]
    for i, v in enumerate(extra):
        strip = jnp.where(row == i, v, strip)
    own_ref[192:] = strip.astype(BF16)
    send_ref[192:] = strip.astype(BF16)


def proj_grads(ins, outs, scr, export):
    idx_ref, o_l, ga_l = ins
    c = idx_ref[0]
    oth, own = outs
    w = scr[0]
    w[...] = mm(o_l.ready()[...], ga_l.ready()[...], TN)
    for i, r in enumerate(DOUBLED):
        base = block_place(idx_ref, r) * T
        mine = pl.ds(pl.multiple_of(base + c * 64, 64), 64)
        other = pl.ds(pl.multiple_of(base + (1 - c) * 64, 64), 64)
        j = DOUBLED.index(r ^ 3 if r % 4 in (1, 2) else r)
        own.ref[64 * i : 64 * i + 64] = w[mine, :].astype(BF16)
        oth[64 * j : 64 * j + 64] = w[other, :].astype(BF16)


def fold(ins, outs, scr, export):
    a, b = ins
    a = a.ready() if isinstance(a, Load) else a
    n = outs[0].shape[0]
    outs[0][...] = a[:n] + b[:n]
    outs[1][...] = a[n:] + b[n:]


def last(ins, outs, scr, export):
    x_ref, dh_l, gains_ref = (v.ready() for v in ins[2:])
    vhat, inv = norm_parts(x_ref[...].astype(F32))
    outs[0][...] = dh_l[...] + norm_back(vhat, inv, total_of(ins[:2]), gains_ref[0:1, :])


def halves_sum(ins, outs, scr, export):
    keep, got = ins[0].ready(), ins[1]
    outs[0].ref[...] = keep[0] + got[0]
    other = keep[1] + got[1]
    outs[1][...] = other[:256]
    outs[2][...] = other[256:]


def ring_blocks(idx_ref, whole, outs, n, extra=None):
    at = lambda i: pl.ds(pl.multiple_of(idx_ref[6 + i] * n, n), n)
    m = n if extra is None else n + extra.shape[0]
    for i, (ref, first) in enumerate(((outs[0], 0), (outs[1], 0), (outs[2], 0), (outs[2], m))):
        ref[first : first + n] = whole[at(i), :]
        if extra is not None:
            ref[first + n : first + m] = extra


def mlp_blocks(ins, outs, scr, export):
    idx_ref, mine, inner, outer = ins
    mine = mine.ready()
    scr[0][:256] = mine[:256] + inner[...]
    scr[0][256:] = mine[256:] + outer[...]
    ring_blocks(idx_ref, scr[0], outs, 128)


def attn_blocks(ins, outs, scr, export):
    idx_ref, own, got, *proj = ins
    scr[0][:192] = own[:192] + got[:192]
    scr[0][192:] = total_of(proj).astype(BF16)
    ring_blocks(idx_ref, scr[0], outs, 64, own[192:] + got[192:])


def spread(ins, outs, scr, export):
    idx_ref = ins[0]
    n = scr[0].shape[1]
    for r in range(4):
        scr[0][idx_ref[6 + r]] = ins[1 + r][:n].astype(F32)
    rows = 0
    for ref in outs:
        for i in range(ref.shape[0] // n):
            export(scr[0].at[rows], ref.at[pl.ds(i * n, n)])
            rows += 1


def data_sum(idx, own, a, got, n, shapes):
    m = own.shape[0]
    mine = own + got[:m] + side_a(a + got[m:], "z")
    mine = mine + lax.ppermute(mine, "yh", SWAP)
    return mine, call(
        spread,
        1,
        [("S", idx)] + [("V", v) for v in ring_gather(mine, "z")],
        [("X", s, F32) for s in shapes],
        scratch=[pltpu.VMEM((4, n, D), F32)],
        exports=4,
    )


def after(values, event):
    return lax.optimization_barrier((*values, event))[: len(values)]


def on_device(x, lengths, gains, wq, wk, wv, wo, wup, wdown, upstream):
    c, yl, xi, z = (lax.axis_index(n) for n in ("c", "yl", "x", "z"))

    def ring(i):
        first, second = i ^ 1, (i + 2 * (i & 1) + 3) & 3
        return [i, jnp.where(c == 0, first, second), jnp.where(c == 0, second, first), i ^ 2]

    idx = jnp.stack([c, yl, *ring(xi), *ring(z)]).astype(jnp.int32)
    freq = (10000.0 ** (-2.0 * np.arange(32) / 64.0)).astype(np.float32)
    freq = jnp.asarray(np.tile(freq, 4)[None, :])
    bf = lambda k, *s: (k, s, BF16)
    f32 = lambda k, *s: (k, s, F32)
    many = lambda k, arrays: [(k, a) for a in arrays]
    I = ("S", idx)
    G, X, U = ("H", gains), ("H", x), ("H", upstream)

    (n1,) = call(first_norm, 1.0, [X, G], [bf("H", T, D)], vmem=60)
    n1 = chip_gather(n1)
    wqkv, w_own = call(
        pack, 1.0, many("R", (wq, wk, wv, wup, wdown)), [bf("V", 192, D), bf("X", 512, D)], exports=5
    )
    wqkv_o = core(wqkv)
    w_core = core(w_own)
    w_y = lax.ppermute(w_own, ("yh", "yl"), OUTER)
    wo_all = stack(wo, side_y(wo))
    wo_all = stack(wo_all, side_a(wo_all, "x"))
    wo_b = side_b(wo_all, "x")
    turn, mask, turn_keep = call(
        tables,
        3,
        [I, ("S", lengths), ("V", freq)],
        [f32("V", 2, OWN, T), bf("H", 3, OWN, T), f32("X", 2, OWN, T)],
        exports=1,
    )
    q, kv, w_pair = call(
        qkv,
        3.0,
        [I, ("V", wqkv), ("V", wqkv_o), ("V", turn)] + many("V", n1),
        [bf("V", OWN, T), bf("V", OWN, 2 * T), bf("H", 3 * T, D)],
    )
    kvo = core(kv)
    q, w_core, w_y = after([q, w_core, w_y], kvo)
    o, o32, lse, q_keep, kv_keep, kvo_keep, n1_all = call(
        attend,
        100.0,
        [I, ("V", q), ("V", kv), ("V", kvo), ("H", mask)] + many("V", n1),
        [
            bf("V", 8, T, T),
            f32("H", T, OWN),
            f32("H", 8, OWN),
            bf("X", OWN, T),
            bf("X", OWN, 2 * T),
            bf("X", OWN, 2 * T),
            bf("X", OWN, D),
        ],
        scratch=[pltpu.VMEM((2, T, OWN), BF16)],
        exports=11,
    )
    (wo_b,) = after([wo_b], o)
    wo_all = stack(wo_all, wo_b)
    (o,) = after([o], wo_all)
    wo_c = core(wo_all)
    o_all = lax.all_to_all(o, ("yl", "x"), 0, 0, tiled=True)
    n2, stat_a, a, h, o_full, wo_full = call(
        middle,
        2.0,
        [I, ("V", o_all), ("V", wo_all), ("V", wo_c), X, G],
        [bf("V", T, D), f32("V", 8, T), f32("H", T, D), f32("H", T, D), bf("H", T, D), bf("H", D, D)],
    )
    (w_y,) = after([w_y], n2)
    ws = many("H", (w_own, w_core, w_y, core(w_y)))
    u, n2_all, *parts = call(
        mlp_forward,
        4.0,
        many("V", ring_gather(n2, "x")) + ws,
        [f32("V", 4 * T, D), bf("X", 4 * T, D)] + [bf("V", T, D)] * 4,
        vmem=24,
        exports=4,
    )
    terms, _ = ring_scatter(parts, "x")
    block_out, gm, dc3, stat_m = call(
        turn_back,
        1.0,
        many("V", terms) + [("H", h), G, U],
        [bf("V", T, D), bf("V", T, D), f32("V", 1, D), f32("V", 8, T)],
    )
    gm = ring_gather(gm, "x")
    zz, du, *parts = call(
        mlp_backward,
        4.0,
        many("V", gm) + ws + [("V", u)],
        [bf("V", 4 * T, D), bf("V", 4 * T, D)] + [bf("V", T, D)] * 4,
        vmem=24,
    )
    terms, passed = ring_scatter(parts, "x")
    zz, du = after([zz, du], passed)
    send, keep = call(
        mlp_grads,
        30.0,
        [("H", n2_all), ("V", zz), ("V", du)] + many("V", gm),
        [bf("V", 2, 512, D), bf("H", 2, 512, D)],
    )
    got = core(send)
    do, dc12, dh, ga = call(
        back_middle,
        30.0,
        many("V", terms) + [("H", h), ("H", a), G, U, ("H", wo_full)],
        [bf("V", 8, T, T), f32("V", 2, D), f32("H", T, D), bf("H", T, D)],
    )
    mine, oa, ob = call(
        halves_sum, 1.0, [("H", keep), ("V", got)], [bf("H", 512, D), bf("V", 256, D), bf("V", 256, D)]
    )
    inner = side_y(oa)
    outer = lax.ppermute(ob, ("yh", "yl"), OUTER)
    (do,) = after([do], oa)
    do_all = lax.all_to_all(do, ("yl", "x"), 0, 0, tiled=True).reshape(OWN, T)
    po_send, po = call(
        proj_grads,
        2.0,
        [I, ("H", o_full), ("H", ga)],
        [bf("V", 512, D), bf("H", 512, D)],
        scratch=[pltpu.VMEM((D, D), F32)],
    )
    po_got = core(po_send)
    po, po_send = call(fold, 1.0, [("H", po), ("V", po_got)], [bf("V", 256, D)] * 2)
    (do_all,) = after([do_all], (oa, po_send))
    po_got = side_b(po_send, "x")
    dq, oth, own32 = call(
        attend_back,
        10,
        [I] + many("H", (do_all, q_keep, kv_keep, kvo_keep, o32, mask, lse, turn_keep)),
        [bf("H", OWN, T), bf("H", OWN, 2 * T), f32("H", OWN, 2 * T)],
        scratch=[pltpu.VMEM((OWN, 2 * T), F32), pltpu.VMEM((2, T, OWN), BF16)],
        vmem=60,
    )
    (oth,) = after([oth], (inner, outer, po_got))
    recv = core(oth)
    inner, outer, po_got = after([inner, outer, po_got], oth)
    m_blocks = call(
        mlp_blocks,
        1.0,
        [I, ("H", mine), ("V", inner), ("V", outer)],
        [bf("V", 128, D), bf("V", 128, D), bf("V", 256, D)],
        scratch=[pltpu.VMEM((512, D), BF16)],
    )
    got_z = side_b(m_blocks[2], "z")
    dqkv, part, part_send = call(
        input_back,
        2.0,
        [I] + many("H", (dq, own32, recv, w_pair, turn_keep)),
        [bf("X", OWN, 3 * T), bf("V", 4 * T, D), bf("V", 4 * T, D)],
        scratch=[pltpu.VMEM((OWN, 3 * T), BF16)],
        exports=1,
    )
    part, part_send = call(
        fold, 1.0, many("V", (part, side_b(part_send, "x"))), [bf("V", 2 * T, D)] * 2
    )
    part, part_send = call(
        fold, 1.0, many("V", (part, side_a(part_send, "x"))), [bf("V", T, D)] * 2
    )
    g_send, g_own = call(
        attn_grads,
        2.0,
        [I, ("H", dqkv), ("H", n1_all), ("H", w_pair), G] + many("V", (dc12, dc3, stat_a, stat_m)),
        [bf("V", 208, D), bf("V", 208, D)],
    )
    g_recv = core(g_send)
    (input_grad,) = call(
        last, 1.0, many("V", (part, side_y(part_send))) + [X, ("H", dh), G], [f32("V", T, D)]
    )
    _, (g_up, g_down) = data_sum(idx, m_blocks[0], m_blocks[1], got_z, 128, [(256, D), (256, D)])

    po, po_send = call(fold, 1.0, many("V", (po, po_got)), [bf("V", 128, D)] * 2)
    po, po_send = call(fold, 1.0, many("V", (po, side_a(po_send, "x"))), [bf("V", 64, D)] * 2)
    blocks = call(
        attn_blocks,
        1.0,
        [I] + many("V", (g_own, g_recv, po, side_y(po_send))),
        [bf("V", 80, D), bf("V", 80, D), bf("V", 160, D)],
        scratch=[pltpu.VMEM((256, D), BF16)],
    )
    mine, (g_q, g_k, g_v, g_o) = data_sum(
        idx, blocks[0], blocks[1], side_b(blocks[2], "z"), 64, [(64, D)] * 4
    )

    rows = mine[64:72].astype(F32)
    rows = rows + side_a(rows, "x")
    rows = rows + side_b(rows, "x")
    rows = rows + side_y(rows)
    stats = rows[4:6, 0] * (1.0 / 16384.0)
    return block_out, input_grad, g_q, g_k, g_v, g_o, g_up, g_down, rows[:4], stats


def solution(mesh):
    names = ("yh", "z", "yl", "x", "c")
    fine = Mesh(np.asarray(mesh.devices).reshape(2, 4, 2, 4, 2), names)
    tokens, group, shard = P(names, None), P(("yh", "z"), None), P(("yl", "x", "c"), None)
    return jax.shard_map(
        on_device,
        mesh=fine,
        in_specs=(tokens, group, P(), shard, shard, shard, shard, shard, shard, tokens),
        out_specs=(tokens, tokens, shard, shard, shard, shard, shard, shard, P(), P()),
        check_vma=False,
    )
```

```python
import functools

import jax
import jax.numpy as jnp
import numpy as np
from jax import lax
from jax.experimental import pallas as pl
from jax.experimental.pallas import tpu as pltpu
from jax.sharding import Mesh
from jax.sharding import PartitionSpec as P

D = 1024
T = 128
NB = 8
OWN = NB * T
F32 = jnp.float32
BF16 = jnp.bfloat16
NEG = -1e30
EPS = 1e-05
MATCH = ([(0, 1), (1, 0), (2, 3), (3, 2)], [(1, 2), (2, 1), (3, 0), (0, 3)])
SIDE_A = [(2 * i + c, 2 * j + c) for c in range(2) for i, j in MATCH[c]]
SIDE_B = [(2 * i + c, 2 * j + c) for c in range(2) for i, j in MATCH[1 - c]]
SWAP = [(0, 1), (1, 0)]
OUTER = [(0, 3), (3, 0), (1, 2), (2, 1)]
NT = (((1,), (1,)), ((), ()))
NN = (((1,), (0,)), ((), ()))
TN = (((0,), (0,)), ((), ()))
GELU_A = float(np.sqrt(2.0 / np.pi))
GELU_B = 0.044715


def mm(a, b, dims=NN):
    return lax.dot_general(a, b, dims, preferred_element_type=F32)


class Load:
    def __init__(self, src, dst, sem):
        self.copy, self.dst, self.waited = pltpu.make_async_copy(src, dst, sem), dst, False
        self.copy.start()

    def ready(self):
        if not self.waited:
            self.copy.wait()
            self.waited = True
        return self.dst


class Store:
    def __init__(self, src, dst, sem):
        self.copy, self.ref, self.sent = pltpu.make_async_copy(src, dst, sem), src, False

    def flush(self):
        if not self.sent:
            self.copy.start()
            self.sent = True


def call(body, us, ins, outs, vmem=16, scratch=(), exports=0):
    space = {"S": pltpu.SMEM, "V": pltpu.VMEM, "H": pltpu.HBM, "X": pltpu.HBM, "R": pltpu.HBM}
    kinds_in, kinds_out = [k for k, _ in ins], [k for k, _, _ in outs]
    buffers = [pltpu.VMEM(a.shape, a.dtype) for k, a in ins if k == "H"]
    buffers += [pltpu.VMEM(s, d) for k, s, d in outs if k == "H"]
    n_sems = len(buffers) + exports

    def kernel(*refs):
        refs = list(refs)
        n_in, n_out = len(ins), len(outs)
        raw_in, raw_out = refs[:n_in], refs[n_in : n_in + n_out]
        held = refs[n_in + n_out : n_in + n_out + len(buffers)]
        rest = refs[n_in + n_out + len(buffers) :]
        if n_sems:
            sems, rest = rest[0], rest[1:]
        used = [0]
        exported = []

        def sem():
            used[0] += 1
            return sems.at[used[0] - 1]

        def export(src, dst):
            copy = pltpu.make_async_copy(src, dst, sem())
            copy.start()
            exported.append(copy)

        held = list(held)
        loads = [Load(r, held.pop(0), sem()) if k == "H" else r for k, r in zip(kinds_in, raw_in)]
        stores = [Store(held.pop(0), r, sem()) if k == "H" else r for k, r in zip(kinds_out, raw_out)]
        body(loads, stores, rest, export)
        for s in stores:
            if isinstance(s, Store):
                s.flush()
        for v in loads:
            if isinstance(v, Load):
                v.ready()
        for s in stores:
            if isinstance(s, Store):
                s.copy.wait()
        for copy in exported:
            copy.wait()

    return pl.pallas_call(
        kernel,
        out_shape=tuple(jax.ShapeDtypeStruct(s, d) for _, s, d in outs),
        in_specs=[pl.BlockSpec(memory_space=space[k]) for k in kinds_in],
        out_specs=tuple(pl.BlockSpec(memory_space=space[k]) for k in kinds_out),
        scratch_shapes=buffers + ([pltpu.SemaphoreType.DMA((n_sems,))] if n_sems else []) + list(scratch),
        compiler_params=pltpu.CompilerParams(vmem_limit_bytes=vmem << 20),
        cost_estimate=pl.CostEstimate(flops=int(us * 1.1e9), bytes_accessed=0, transcendentals=0),
    )(*[a for _, a in ins])


def side_a(v, axis):
    return lax.ppermute(v, (axis, "c"), SIDE_A)


def side_b(v, axis):
    return lax.ppermute(v, (axis, "c"), SIDE_B)


def side_y(v):
    return lax.ppermute(v, "yl", SWAP)


def core(v):
    return lax.ppermute(v, "c", SWAP)


def ring_gather(own, axis):
    a = side_a(own, axis)
    b = side_b(own, axis)
    return [own, a, b, side_b(a, axis)]


def ring_scatter(parts, axis):
    own, a, b, f = parts
    got = side_b(f, axis)
    other = side_b(b, axis)
    passed = a + got
    return [own, other, side_a(passed, axis)], passed


def chip_gather(own):
    y = side_y(own)
    row = ring_gather(own, "x")
    return row + [y, side_a(y, "x"), side_b(y, "x"), side_y(row[3])]


def norm_parts(v):
    center = v - jnp.mean(v, axis=-1, keepdims=True)
    inv = lax.rsqrt(jnp.mean(center * center, axis=-1, keepdims=True) + EPS)
    return center * inv, inv


def norm_back(vhat, inv, grad, gain):
    t = grad * gain
    return inv * (
        t
        - jnp.mean(t, axis=-1, keepdims=True)
        - vhat * jnp.mean(t * vhat, axis=-1, keepdims=True)
    )


def first_norm(ins, outs, scr, export):
    x, gains = (v.ready() for v in ins)
    vhat, _ = norm_parts(x[...].astype(F32))
    outs[0].ref[...] = (vhat * gains[0:1, :]).astype(BF16)


def stack(*arrays):
    rows = [v.shape[0] for v in arrays]

    def body(ins, outs, scr, export):
        at = 0
        for ref, n in zip(ins, rows):
            outs[0][at : at + n] = ref[...]
            at += n

    return call(body, 1, [("V", v) for v in arrays], [("V", (sum(rows), D), BF16)])[0]


def pack(ins, outs, scr, export):
    at = [0, 0]
    for i, ref in enumerate(ins):
        o = 0 if i < 3 else 1
        export(ref, outs[o].at[pl.ds(at[o], ref.shape[0])])
        at[o] += ref.shape[0]


def own_places(parity, rows):
    i = lax.broadcasted_iota(jnp.int32, (rows, T), 0)
    return ((i // T) * 2 + parity) * T + i % T


def row_of(ends_ref, places):
    row = jnp.zeros_like(places)
    start = jnp.zeros_like(places)
    end = jnp.int32(0)
    for k in range(8):
        end = end + ends_ref[0, k]
        inside = places >= end
        row = row + jnp.where(inside, 1, 0)
        start = jnp.where(inside, end, start)
    return row, places - start


def tables(ins, outs, scr, export):
    idx_ref, len_ref, freq_ref = ins
    turn, mask_out, turn_keep = outs
    c = idx_ref[0]
    n = OWN // 4
    lane = lax.broadcasted_iota(jnp.int32, (n, T), 1)
    token = lax.broadcasted_iota(jnp.int32, (n, T), 0) + (lane // 32) * n
    _, pos = row_of(len_ref, ((token // T) * 2 + c) * T + token % T)
    angle = pos.astype(F32) * freq_ref[...]
    for i, v in enumerate((jnp.cos(angle), jnp.sin(angle))):
        for g in range(4):
            w = jnp.where(lane // 32 == g, v, 0.0)
            w = w + pltpu.roll(w, 32, 1)
            w = w + pltpu.roll(w, 64, 1)
            if i == 1:
                w = jnp.where(lane % 64 < 32, -w, w)
            turn[i, n * g : n * g + n] = w
    export(turn, turn_keep)
    lane = lax.broadcasted_iota(jnp.int32, (OWN, T), 1)
    row, _ = row_of(len_ref, own_places(c, OWN))
    mask_out.ref[0] = jnp.where((lane < 8) & (lane != row), NEG, 0.0).astype(BF16)
    mask_out.ref[1] = jnp.where(lane == row, 1.0, 0.0).astype(BF16)
    row, _ = row_of(len_ref, own_places(1 - c, OWN))
    mask_out.ref[2] = jnp.where(lane == row, 1.0, 0.0).astype(BF16)


def swap_halves(w):
    lane = lax.broadcasted_iota(jnp.int32, w.shape, 1)
    return jnp.where(lane % 64 < 32, pltpu.roll(w, 96, 1), pltpu.roll(w, 32, 1))


def pair_rows(c, own, other):
    first = jnp.where(c == 0, own, other)
    second = jnp.where(c == 0, other, own)
    return jnp.concatenate([first, second], 0)


def block_place(idx_ref, r):
    yl = idx_ref[1] if r < 4 else 1 - idx_ref[1]
    return yl * 4 + idx_ref[2 + r % 4]


def qkv(ins, outs, scr, export):
    idx_ref, own_ref, other_ref, turn = ins[:4]
    blocks = ins[4:]
    q_ref, kv_ref, w_out = outs
    c = idx_ref[0]
    w = jnp.concatenate(
        [
            pair_rows(c, own_ref[64 * i : 64 * i + 64], other_ref[64 * i : 64 * i + 64])
            for i in range(3)
        ],
        0,
    )
    w_out.ref[...] = w
    w_out.flush()
    for half in (0, 4):
        out = mm(jnp.concatenate([v[...] for v in blocks[half : half + 4]], 0), w, NT)
        for i in range(4):
            rows = pl.ds(pl.multiple_of(block_place(idx_ref, half + i) * T, T), T)
            part = out[T * i : T * i + T]
            cos, sin = turn[0, rows, :], turn[1, rows, :]
            q, k = part[:, :T], part[:, T : 2 * T]
            q_ref[rows, :] = ((q * cos + swap_halves(q) * sin) * 0.125).astype(BF16)
            kv_ref[rows, :T] = (k * cos + swap_halves(k) * sin).astype(BF16)
            kv_ref[rows, T:] = part[:, 2 * T :].astype(BF16)


Q = 256


def head_lanes(w):
    lane = lax.broadcasted_iota(jnp.int32, w.shape, 1)
    fill = jnp.zeros_like(w)
    return jnp.where(lane < 64, w, fill), jnp.where(lane < 64, fill, w)


def diag_masks(c):
    k = lax.broadcasted_iota(jnp.int32, (Q, Q), 0)
    i = lax.broadcasted_iota(jnp.int32, (Q, Q), 1)
    kb, ib = k // T, i // T
    return k <= i, (kb < ib) | ((kb == ib) & (c == 1))


def visible(s, masks, other):
    n = s.shape[0] // 2
    own = jnp.where(masks[0], s[n - Q : n], other)
    parts = [own, jnp.where(masks[1], s[2 * n - Q :], other)]
    if n > Q:
        parts = [s[: n - Q], parts[0], s[n : 2 * n - Q], parts[1]]
    return jnp.concatenate(parts, 0)


def both_keys(kv_ref, kvo_ref, mask, rows):
    own = jnp.concatenate([kv_ref[rows, :T], mask[1, rows, :]], 1)
    other = jnp.concatenate([kvo_ref[rows, :T], mask[2, rows, :]], 1)
    return jnp.concatenate([own, other], 0)


def turned(w):
    return w.astype(F32).T.astype(BF16)


def attend(ins, outs, scr, export):
    idx_ref, q_ref, kv_ref, kvo_ref, mask = ins[:5]
    o_ref, o_keep, lse, q_keep, kv_keep, kvo_keep, n_keep = outs
    (vt,) = scr
    export(q_ref, q_keep)
    export(kv_ref, kv_keep)
    export(kvo_ref, kvo_keep)
    for r in range(8):
        export(ins[5 + r], n_keep.at[pl.ds(pl.multiple_of(block_place(idx_ref, r) * T, T), T)])
    for i, kv in enumerate((kv_ref, kvo_ref)):
        for b in range(OWN // Q):
            vt[i, :, Q * b : Q * b + Q] = turned(kv[Q * b : Q * b + Q, T:])
    mask = mask.ready()
    masks = diag_masks(idx_ref[0])
    ones = jnp.ones((16, 2 * Q), BF16)

    for jt in range(OWN // Q):
        qrows = slice(jt * Q, jt * Q + Q)
        mq = mask[0, qrows, :]
        qa = [jnp.concatenate([h, mq], 1) for h in head_lanes(q_ref[qrows, :])]

        def tile(it, state, diag):
            rows = slice(it * Q, it * Q + Q)
            v = jnp.concatenate([vt[0, :, rows], vt[1, :, rows]], 1)
            k = [
                jnp.concatenate([kv[rows, :T], mask[1 + i, rows, :]], 1)
                for i, kv in enumerate((kv_ref, kvo_ref))
            ]
            out = []
            for h in range(2):
                m, acc = state[h]
                s = [mm(k[i], qa[h], NT) for i in range(2)]
                if diag:
                    s = [jnp.where(masks[i], s[i], NEG) for i in range(2)]
                top = jnp.max(jnp.maximum(s[0], s[1]), axis=0, keepdims=True)
                m_new = jnp.maximum(m, top)
                p = jnp.concatenate([jnp.exp(v_ - m_new).astype(BF16) for v_ in s], 0)
                vh = jnp.concatenate([v[64 * h : 64 * h + 64], ones], 0)
                out.append((m_new, acc * jnp.exp(m - m_new) + mm(vh, p)))
            return tuple(out)

        zero = (jnp.full((1, Q), NEG, F32), jnp.zeros((80, Q), F32))
        state = tile(jt, (zero, zero), True)
        for it in range(jt):
            state = tile(it, state, False)
        o = jnp.concatenate([acc[:64] / acc[64:65] for _, acc in state], 0)
        o_keep.ref[:, qrows] = o
        o = o.T.astype(BF16)
        for b in range(Q // T):
            o_ref[jt * (Q // T) + b] = o[b * T : b * T + T]
        for h, (m, acc) in enumerate(state):
            lse.ref[h : h + 1, qrows] = m + jnp.log(acc[64:65])


DOUBLED = [0, 4, 1, 5, 2, 6, 3, 7]


def middle(ins, outs, scr, export):
    idx_ref, o_ref, own_ref, other_ref, x_l, gains_l = ins
    n2_ref, stat_ref, a_out, h_out, o_out, w_out = outs
    c = idx_ref[0]
    o = jnp.concatenate([o_ref[j] for j in range(8)], 1)
    o_out.ref[...] = o
    o_out.flush()
    for i, r in enumerate(DOUBLED):
        rows = pl.ds(pl.multiple_of(block_place(idx_ref, r) * T, T), T)
        j = DOUBLED.index(r ^ 3 if r % 4 in (1, 2) else r)
        part, part_o = slice(64 * i, 64 * i + 64), slice(64 * j, 64 * j + 64)
        w_out.ref[rows, :] = pair_rows(c, own_ref[part], other_ref[part_o])
    w_out.flush()
    a = mm(o, w_out.ref[...])
    a_out.ref[...] = a
    a_out.flush()
    vhat, _ = norm_parts(a)
    x_ref, gains_ref = x_l.ready(), gains_l.ready()
    h = x_ref[...].astype(F32) + vhat * gains_ref[1:2, :]
    h_out.ref[...] = h
    h_out.flush()
    vhat, _ = norm_parts(h)
    n2_ref[...] = (vhat * gains_ref[2:3, :]).astype(BF16)
    stat_ref[...] = jnp.zeros((8, T), F32) + jnp.sum(a * a) * (1.0 / D)


def gelu_tanh(u):
    return jnp.tanh(GELU_A * (u + GELU_B * u * u * u))


def mlp_forward(ins, outs, scr, export):
    ns, ws = ins[:4], ins[4:8]
    u_ref, n_out, parts = outs[0], outs[1], outs[2:]
    for i, ref in enumerate(ns):
        export(ref, n_out.at[pl.ds(T * i, T)])
    n = jnp.concatenate([r[...] for r in ns], 0)
    zs = []
    for s in range(4):
        u = mm(n, ws[s].ready()[:256], NT)
        u_ref[:, 256 * s : 256 * s + 256] = u
        zs.append((0.5 * u * (1.0 + gelu_tanh(u))).astype(BF16))
    m = mm(jnp.concatenate(zs, 1), jnp.concatenate([w.ready()[256:] for w in ws], 0))
    for i in range(4):
        parts[i][...] = m[T * i : T * i + T].astype(BF16)


def total_of(refs):
    total = refs[0][...].astype(F32)
    for ref in refs[1:]:
        total = total + ref[...].astype(F32)
    return total


def turn_back(ins, outs, scr, export):
    h_ref, gains_ref, up_ref = (v.ready() for v in ins[3:])
    out_ref, g_ref, dc_ref, stat_ref = outs
    m = total_of(ins[:3])
    vhat, inv = norm_parts(m)
    gain = gains_ref[3:4, :]
    dy = up_ref[...].astype(F32)
    g_ref[...] = norm_back(vhat, inv, dy, gain).astype(BF16)
    dc_ref[...] = jnp.sum(dy * vhat, axis=0, keepdims=True)
    stat_ref[...] = jnp.zeros((8, T), F32) + jnp.sum(m * m) * (1.0 / D)
    out_ref[...] = (h_ref[...] + vhat * gain).astype(BF16)


def mlp_slopes(ins, outs, scr, export):
    z_ref, slope_ref = outs
    u = ins[0][...]
    t = gelu_tanh(u)
    z_ref[...] = (0.5 * u * (1.0 + t)).astype(BF16)
    slope_ref[...] = 0.5 * (1.0 + t) + 0.5 * u * (1.0 - t * t) * GELU_A * (
        1.0 + 3.0 * GELU_B * u * u
    )


def mlp_backward(ins, outs, scr, export):
    gs, ws, slope_ref = ins[:4], ins[4:8], ins[8]
    du_ref, parts = outs[0], outs[1:]
    g = jnp.concatenate([r[...] for r in gs], 0)
    for s in range(4):
        cols = slice(256 * s, 256 * s + 256)
        du = mm(g, ws[s].ready()[256:], NT) * slope_ref[:, cols]
        du_ref[:, cols] = du.astype(BF16)
    dn = mm(du_ref[...], jnp.concatenate([w.ready()[:256] for w in ws], 0))
    for i in range(4):
        parts[i][...] = dn[T * i : T * i + T].astype(BF16)


def mlp_grads(ins, outs, scr, export):
    n_l, z, du, gs = ins[0], ins[1], ins[2], ins[3:]
    send_ref, keep = outs
    g = jnp.concatenate([r[...] for r in gs], 0)
    n = n_l.ready()[...]
    for s, ref, slot in ((1, send_ref, 0), (3, send_ref, 1), (0, keep.ref, 0), (2, keep.ref, 1)):
        cols = slice(256 * s, 256 * s + 256)
        ref[slot, :256] = mm(du[:, cols], n, TN).astype(BF16)
        ref[slot, 256:] = mm(z[:, cols], g, TN).astype(BF16)


def back_middle(ins, outs, scr, export):
    h_ref, a_ref, gains_l, up_l, wo_ref = ins[3:]
    gains_ref, up_ref = gains_l.ready(), up_l.ready()
    do_ref, dc_ref, dh_out, ga_out = outs
    dn = total_of(ins[:3])
    vhat, inv = norm_parts(h_ref.ready()[...])
    dc_ref[1:2, :] = jnp.sum(dn * vhat, axis=0, keepdims=True)
    dh = up_ref[...].astype(F32) + norm_back(vhat, inv, dn, gains_ref[2:3, :])
    dh_out.ref[...] = dh
    dh_out.flush()
    vhat, inv = norm_parts(a_ref.ready()[...])
    dc_ref[0:1, :] = jnp.sum(dh * vhat, axis=0, keepdims=True)
    ga = norm_back(vhat, inv, dh, gains_ref[1:2, :]).astype(BF16)
    ga_out.ref[...] = ga
    ga_out.flush()
    do = mm(ga, wo_ref.ready()[...], NT).astype(BF16)
    for j in range(8):
        do_ref[j] = do[:, T * j : T * j + T]


def attend_back(ins, outs, scr, export):
    idx_ref = ins[0]
    do_ref, q_ref, kv_ref, kvo_ref, o_ref, mask, lse, tab = ins[1:]
    dq_out, oth_out, own_out = outs
    acco, kt = scr
    own_ref = own_out.ref
    kv_ref, kvo_ref, mask = kv_ref.ready(), kvo_ref.ready(), mask.ready()
    for i, kv in enumerate((kv_ref, kvo_ref)):
        for b in range(OWN // Q):
            kt[i, :, Q * b : Q * b + Q] = turned(kv[Q * b : Q * b + Q, :T])
    own_ref[...] = jnp.zeros_like(own_ref)
    acco[...] = jnp.zeros_like(acco)
    masks = diag_masks(idx_ref[0])
    do_ref, q_ref, o_ref, lse, tab = (v.ready() for v in (do_ref, q_ref, o_ref, lse, tab))

    for jt in range(OWN // Q):
        qrows = slice(jt * Q, jt * Q + Q)
        do = do_ref[qrows, :]
        q_h, do_h = head_lanes(q_ref[qrows, :]), head_lanes(do)
        mq = mask[0, qrows, :]
        qa = [jnp.concatenate([h, mq], 1) for h in q_h]
        inner = do.astype(F32).T * o_ref[:, qrows]
        delta = [jnp.sum(inner[64 * h : 64 * h + 64], axis=0, keepdims=True) for h in range(2)]
        top = [lse[h : h + 1, qrows] for h in range(2)]
        q_st, do_st = jnp.concatenate(q_h, 0), jnp.concatenate(do_h, 0)

        n = jt * Q + Q
        k = both_keys(kv_ref, kvo_ref, mask, slice(0, n))
        v = jnp.concatenate([kv_ref[:n, T:], kvo_ref[:n, T:]], 0)
        t = jnp.concatenate([kt[0, :, :n], kt[1, :, :n]], 1)
        ps, ss, dq = [], [], []
        for h in range(2):
            p = visible(jnp.exp(mm(k, qa[h], NT) - top[h]), masks, 0.0)
            s = (p * (mm(v, do_h[h], NT) - delta[h])).astype(BF16)
            ps.append(p.astype(BF16))
            ss.append(s)
            dq.append(mm(t[64 * h : 64 * h + 64], s))
        dk = mm(jnp.concatenate(ss, 1), q_st)
        dv = mm(jnp.concatenate(ps, 1), do_st)
        own_ref[:n, :T] += dk[:n]
        own_ref[:n, T:] += dv[:n]
        acco[:n, :T] += dk[n:]
        acco[:n, T:] += dv[n:]
        dq = jnp.concatenate(dq, 0).T * 0.125
        dq_out.ref[qrows, :] = (
            dq * tab[0, qrows, :] + swap_halves(dq * tab[1, qrows, :])
        ).astype(BF16)

    own_out.flush()
    dq_out.flush()
    oth_out.ref[...] = acco[...].astype(BF16)


def input_back(ins, outs, scr, export):
    idx_ref = ins[0]
    dq_ref, own_ref, recv_ref, w_l, turn_l = ins[1:]
    dq_ref, own_ref, recv_ref = dq_ref.ready(), own_ref.ready(), recv_ref.ready()
    g_ref = scr[0]
    g_out, parts = outs[0], outs[1:]
    tab = turn_l.ready()
    both = own_ref[...] + recv_ref[...].astype(F32)
    dk = both[:, :T]
    g_ref[:, :T] = dq_ref[...]
    g_ref[:, T : 2 * T] = (dk * tab[0] + swap_halves(dk * tab[1])).astype(BF16)
    g_ref[:, 2 * T :] = both[:, T:].astype(BF16)
    export(g_ref, g_out)
    w = w_l.ready()[...]
    for half in (4, 0):
        rows = [
            pl.ds(pl.multiple_of(block_place(idx_ref, r) * T, T), T)
            for r in DOUBLED[half : half + 4]
        ]
        out = mm(jnp.concatenate([g_ref[r, :] for r in rows], 0), w)
        parts[half // 4][...] = out.astype(BF16)


def attn_grads(ins, outs, scr, export):
    idx_ref, g_l, n_l, w_l, gains_l, dc12_ref, dc3_ref, stat_a, stat_m = ins
    gains_ref = gains_l.ready()
    send_ref, own_ref = outs
    c = idx_ref[0]
    g, n, w_ref = g_l.ready(), n_l.ready(), w_l.ready()
    dc = jnp.zeros((1, D), F32)
    for i in range(3):
        w = mm(g[:, T * i : T * i + T], n[...], TN)
        dc = dc + jnp.sum(w * w_ref[T * i : T * i + T, :].astype(F32), axis=0, keepdims=True)
        own_ref[64 * i : 64 * i + 64] = jnp.where(c == 0, w[:64], w[64:]).astype(BF16)
        send_ref[64 * i : 64 * i + 64] = jnp.where(c == 0, w[64:], w[:64]).astype(BF16)
    row = lax.broadcasted_iota(jnp.int32, (16, D), 0)
    strip = jnp.zeros((16, D), F32)
    extra = [dc / gains_ref[0:1, :], dc12_ref[0:1, :], dc12_ref[1:2, :], dc3_ref[...]]
    extra += [stat_a[0:1, 0:1], stat_m[0:1, 0:1]]
    for i, v in enumerate(extra):
        strip = jnp.where(row == i, v, strip)
    own_ref[192:] = strip.astype(BF16)
    send_ref[192:] = strip.astype(BF16)


def proj_grads(ins, outs, scr, export):
    idx_ref, o_l, ga_l = ins
    c = idx_ref[0]
    oth, own = outs
    w = scr[0]
    w[...] = mm(o_l.ready()[...], ga_l.ready()[...], TN)
    for i, r in enumerate(DOUBLED):
        base = block_place(idx_ref, r) * T
        mine = pl.ds(pl.multiple_of(base + c * 64, 64), 64)
        other = pl.ds(pl.multiple_of(base + (1 - c) * 64, 64), 64)
        j = DOUBLED.index(r ^ 3 if r % 4 in (1, 2) else r)
        own.ref[64 * i : 64 * i + 64] = w[mine, :].astype(BF16)
        oth[64 * j : 64 * j + 64] = w[other, :].astype(BF16)


def fold(ins, outs, scr, export):
    a, b = ins
    a = a.ready() if isinstance(a, Load) else a
    n = outs[0].shape[0]
    outs[0][...] = a[:n] + b[:n]
    outs[1][...] = a[n:] + b[n:]


def last(ins, outs, scr, export):
    x_ref, dh_l, gains_ref = (v.ready() for v in ins[2:])
    vhat, inv = norm_parts(x_ref[...].astype(F32))
    outs[0][...] = dh_l[...] + norm_back(vhat, inv, total_of(ins[:2]), gains_ref[0:1, :])


def halves_sum(ins, outs, scr, export):
    keep, got = ins[0].ready(), ins[1]
    outs[0].ref[...] = keep[0] + got[0]
    other = keep[1] + got[1]
    outs[1][...] = other[:256]
    outs[2][...] = other[256:]


def ring_blocks(idx_ref, whole, outs, n, extra=None):
    at = lambda i: pl.ds(pl.multiple_of(idx_ref[6 + i] * n, n), n)
    m = n if extra is None else n + extra.shape[0]
    for i, (ref, first) in enumerate(((outs[0], 0), (outs[1], 0), (outs[2], 0), (outs[2], m))):
        ref[first : first + n] = whole[at(i), :]
        if extra is not None:
            ref[first + n : first + m] = extra


def mlp_blocks(ins, outs, scr, export):
    idx_ref, mine, inner, outer = ins
    mine = mine.ready()
    scr[0][:256] = mine[:256] + inner[...]
    scr[0][256:] = mine[256:] + outer[...]
    ring_blocks(idx_ref, scr[0], outs, 128)


def attn_blocks(ins, outs, scr, export):
    idx_ref, own, got, *proj = ins
    scr[0][:192] = own[:192] + got[:192]
    scr[0][192:] = total_of(proj).astype(BF16)
    ring_blocks(idx_ref, scr[0], outs, 64, own[192:] + got[192:])


def spread(ins, outs, scr, export):
    idx_ref = ins[0]
    n = scr[0].shape[1]
    for r in range(4):
        scr[0][idx_ref[6 + r]] = ins[1 + r][:n].astype(F32)
    rows = 0
    for ref in outs:
        for i in range(ref.shape[0] // n):
            export(scr[0].at[rows], ref.at[pl.ds(i * n, n)])
            rows += 1


def data_sum(idx, own, a, got, n, shapes):
    m = own.shape[0]
    mine = own + got[:m] + side_a(a + got[m:], "z")
    mine = mine + lax.ppermute(mine, "yh", SWAP)
    return mine, call(
        spread,
        1,
        [("S", idx)] + [("V", v) for v in ring_gather(mine, "z")],
        [("X", s, F32) for s in shapes],
        scratch=[pltpu.VMEM((4, n, D), F32)],
        exports=4,
    )


def after(values, event):
    return lax.optimization_barrier((*values, event))[: len(values)]


def on_device(x, lengths, gains, wq, wk, wv, wo, wup, wdown, upstream):
    c, yl, xi, z = (lax.axis_index(n) for n in ("c", "yl", "x", "z"))

    def ring(i):
        first, second = i ^ 1, (i + 2 * (i & 1) + 3) & 3
        return [i, jnp.where(c == 0, first, second), jnp.where(c == 0, second, first), i ^ 2]

    idx = jnp.stack([c, yl, *ring(xi), *ring(z)]).astype(jnp.int32)
    freq = (10000.0 ** (-2.0 * np.arange(32) / 64.0)).astype(np.float32)
    freq = jnp.asarray(np.tile(freq, 4)[None, :])
    bf = lambda k, *s: (k, s, BF16)
    f32 = lambda k, *s: (k, s, F32)
    many = lambda k, arrays: [(k, a) for a in arrays]
    I = ("S", idx)
    G, X, U = ("H", gains), ("H", x), ("H", upstream)

    (n1,) = call(first_norm, 1.0, [X, G], [bf("H", T, D)], vmem=60)
    n1 = chip_gather(n1)
    wqkv, w_own = call(
        pack, 1.0, many("R", (wq, wk, wv, wup, wdown)), [bf("V", 192, D), bf("X", 512, D)], exports=5
    )
    wqkv_o = core(wqkv)
    w_core = core(w_own)
    w_y = lax.ppermute(w_own, ("yh", "yl"), OUTER)
    wo_all = stack(wo, side_y(wo))
    wo_all = stack(wo_all, side_a(wo_all, "x"))
    wo_b = side_b(wo_all, "x")
    turn, mask, turn_keep = call(
        tables,
        3,
        [I, ("S", lengths), ("V", freq)],
        [f32("V", 2, OWN, T), bf("H", 3, OWN, T), f32("X", 2, OWN, T)],
        exports=1,
    )
    q, kv, w_pair = call(
        qkv,
        3.0,
        [I, ("V", wqkv), ("V", wqkv_o), ("V", turn)] + many("V", n1),
        [bf("V", OWN, T), bf("V", OWN, 2 * T), bf("H", 3 * T, D)],
    )
    kvo = core(kv)
    q, w_core, w_y = after([q, w_core, w_y], kvo)
    o, o32, lse, q_keep, kv_keep, kvo_keep, n1_all = call(
        attend,
        100.0,
        [I, ("V", q), ("V", kv), ("V", kvo), ("H", mask)] + many("V", n1),
        [
            bf("V", 8, T, T),
            f32("H", T, OWN),
            f32("H", 8, OWN),
            bf("X", OWN, T),
            bf("X", OWN, 2 * T),
            bf("X", OWN, 2 * T),
            bf("X", OWN, D),
        ],
        scratch=[pltpu.VMEM((2, T, OWN), BF16)],
        exports=11,
    )
    (wo_b,) = after([wo_b], o)
    wo_all = stack(wo_all, wo_b)
    (o,) = after([o], wo_all)
    wo_c = core(wo_all)
    o_all = lax.all_to_all(o, ("yl", "x"), 0, 0, tiled=True)
    n2, stat_a, a, h, o_full, wo_full = call(
        middle,
        2.0,
        [I, ("V", o_all), ("V", wo_all), ("V", wo_c), X, G],
        [bf("V", T, D), f32("V", 8, T), f32("H", T, D), f32("H", T, D), bf("H", T, D), bf("H", D, D)],
    )
    (w_y,) = after([w_y], n2)
    ws = many("H", (w_own, w_core, w_y, core(w_y)))
    u, n2_all, *parts = call(
        mlp_forward,
        4.0,
        many("V", ring_gather(n2, "x")) + ws,
        [f32("V", 4 * T, D), bf("X", 4 * T, D)] + [bf("V", T, D)] * 4,
        vmem=24,
        exports=4,
    )
    terms, passed = ring_scatter(parts, "x")
    (u,) = after([u], passed)
    zz, slope = call(
        mlp_slopes,
        20,
        [("V", u)],
        [bf("V", 4 * T, D), f32("V", 4 * T, D)],
    )
    block_out, gm, dc3, stat_m = call(
        turn_back,
        1.0,
        many("V", terms) + [("H", h), G, U],
        [bf("V", T, D), bf("V", T, D), f32("V", 1, D), f32("V", 8, T)],
    )
    gm = ring_gather(gm, "x")
    du, *parts = call(
        mlp_backward,
        4.0,
        many("V", gm) + ws + [("V", slope)],
        [bf("V", 4 * T, D)] + [bf("V", T, D)] * 4,
        vmem=24,
    )
    terms, passed = ring_scatter(parts, "x")
    zz, du = after([zz, du], passed)
    send, keep = call(
        mlp_grads,
        30.0,
        [("H", n2_all), ("V", zz), ("V", du)] + many("V", gm),
        [bf("V", 2, 512, D), bf("H", 2, 512, D)],
    )
    got = core(send)
    do, dc12, dh, ga = call(
        back_middle,
        30.0,
        many("V", terms) + [("H", h), ("H", a), G, U, ("H", wo_full)],
        [bf("V", 8, T, T), f32("V", 2, D), f32("H", T, D), bf("H", T, D)],
    )
    mine, oa, ob = call(
        halves_sum, 1.0, [("H", keep), ("V", got)], [bf("H", 512, D), bf("V", 256, D), bf("V", 256, D)]
    )
    inner = side_y(oa)
    outer = lax.ppermute(ob, ("yh", "yl"), OUTER)
    (do,) = after([do], oa)
    do_all = lax.all_to_all(do, ("yl", "x"), 0, 0, tiled=True).reshape(OWN, T)
    po_send, po = call(
        proj_grads,
        2.0,
        [I, ("H", o_full), ("H", ga)],
        [bf("V", 512, D), bf("H", 512, D)],
        scratch=[pltpu.VMEM((D, D), F32)],
    )
    po_got = core(po_send)
    po, po_send = call(fold, 1.0, [("H", po), ("V", po_got)], [bf("V", 256, D)] * 2)
    (do_all,) = after([do_all], (oa, po_send))
    po_got = side_b(po_send, "x")
    dq, oth, own32 = call(
        attend_back,
        10,
        [I] + many("H", (do_all, q_keep, kv_keep, kvo_keep, o32, mask, lse, turn_keep)),
        [bf("H", OWN, T), bf("H", OWN, 2 * T), f32("H", OWN, 2 * T)],
        scratch=[pltpu.VMEM((OWN, 2 * T), F32), pltpu.VMEM((2, T, OWN), BF16)],
        vmem=60,
    )
    (oth,) = after([oth], (inner, outer, po_got))
    recv = core(oth)
    inner, outer, po_got = after([inner, outer, po_got], oth)
    m_blocks = call(
        mlp_blocks,
        1.0,
        [I, ("H", mine), ("V", inner), ("V", outer)],
        [bf("V", 128, D), bf("V", 128, D), bf("V", 256, D)],
        scratch=[pltpu.VMEM((512, D), BF16)],
    )
    got_z = side_b(m_blocks[2], "z")
    dqkv, part, part_send = call(
        input_back,
        30,
        [I] + many("H", (dq, own32, recv, w_pair, turn_keep)),
        [bf("X", OWN, 3 * T), bf("V", 4 * T, D), bf("V", 4 * T, D)],
        scratch=[pltpu.VMEM((OWN, 3 * T), BF16)],
        exports=1,
    )
    part, part_send = call(
        fold, 1.0, many("V", (part, side_b(part_send, "x"))), [bf("V", 2 * T, D)] * 2
    )
    part, part_send = call(
        fold, 1.0, many("V", (part, side_a(part_send, "x"))), [bf("V", T, D)] * 2
    )
    g_send, g_own = call(
        attn_grads,
        30,
        [I, ("H", dqkv), ("H", n1_all), ("H", w_pair), G] + many("V", (dc12, dc3, stat_a, stat_m)),
        [bf("V", 208, D), bf("V", 208, D)],
    )
    g_recv = core(g_send)
    (input_grad,) = call(
        last, 1.0, many("V", (part, side_y(part_send))) + [X, ("H", dh), G], [f32("V", T, D)]
    )
    _, (g_up, g_down) = data_sum(idx, m_blocks[0], m_blocks[1], got_z, 128, [(256, D), (256, D)])

    po, po_send = call(fold, 1.0, many("V", (po, po_got)), [bf("V", 128, D)] * 2)
    po, po_send = call(fold, 1.0, many("V", (po, side_a(po_send, "x"))), [bf("V", 64, D)] * 2)
    blocks = call(
        attn_blocks,
        20,
        [I] + many("V", (g_own, g_recv, po, side_y(po_send))),
        [bf("V", 80, D), bf("V", 80, D), bf("V", 160, D)],
        scratch=[pltpu.VMEM((256, D), BF16)],
    )
    mine, (g_q, g_k, g_v, g_o) = data_sum(
        idx, blocks[0], blocks[1], side_b(blocks[2], "z"), 64, [(64, D)] * 4
    )

    rows = mine[64:72].astype(F32)
    rows = rows + side_a(rows, "x")
    rows = rows + side_b(rows, "x")
    rows = rows + side_y(rows)
    stats = rows[4:6, 0] * (1.0 / 16384.0)
    return block_out, input_grad, g_q, g_k, g_v, g_o, g_up, g_down, rows[:4], stats


def solution(mesh):
    names = ("yh", "z", "yl", "x", "c")
    fine = Mesh(np.asarray(mesh.devices).reshape(2, 4, 2, 4, 2), names)
    tokens, group, shard = P(names, None), P(("yh", "z"), None), P(("yl", "x", "c"), None)
    return jax.shard_map(
        on_device,
        mesh=fine,
        in_specs=(tokens, group, P(), shard, shard, shard, shard, shard, shard, tokens),
        out_specs=(tokens, tokens, shard, shard, shard, shard, shard, shard, P(), P()),
        check_vma=False,
    )
```
